32 devices in a mesh: tm: 8 (over z, core), space: 4 (over y, x).
Axes of the slice: x: 2, y: 2, z: 4, core: 2. Of those that a mesh axis runs over, the one named last changes fastest.
Arguments:
- initial: float32 [2, 128, 512], P(None, 'space'), may hold values from 0.2 to 1
- guess: float32 [128, 2, 128, 512], P('tm', None, 'space'), may hold values from 0 to 1
- kappa: float32 [2, 128, 512], P(None, 'space'), may hold values from 0.005 to 0.05
- feed: float32 [128, 512], P('space'), may hold values from 0.002 to 0.01
- kill: float32 [128, 512], P('space'), may hold values from 0.002 to 0.008
- react: float32 [128, 512], P('space'), may hold values from 0.002 to 0.008
Outputs:
- solution: float32 [128, 2, 128, 512], P('tm', None, 'space')
The draws below stay inside these ranges and needn't reach their ends.
All inputs are finite; a program needn't handle non-finite values.
Results may differ from the reference program's by a relative error of at most 0.00002.
Values sent between devices are 32-bit elements; how exact they have to be, the bound alone decides.
A program may use at most 128 MiB of HBM per device.

```python
import math
import jax
import jax.numpy as jnp
from jax import lax

COLS = 512
SPAN = 8
NX = 128
NT = 128


def shard_levels(stream_key, extent, pieces, least, high):
    loudness = 1.0
    for dim, blocks in pieces:
        draws = jax.random.uniform(jax.random.fold_in(jax.random.fold_in(stream_key, 6), dim), (blocks,), jnp.float32, least / len(pieces), high / len(pieces))
        loudness = loudness * jnp.repeat(jnp.exp(draws), extent[dim] // blocks).reshape((-1,) + (1,) * (len(extent) - 1 - dim))
    return loudness


def setup_inputs(seed: int = 0) -> dict:
    streams_of = jax.random.split(jax.random.key(seed), 7)
    return {
        "initial": jnp.clip(0.2 + 0.8 * jax.random.uniform(streams_of[0], (2, NX, COLS), jnp.float32) ** shard_levels(streams_of[0], (2, NX, COLS), ((1, 4),), -0.2, 0.2), 0.2, 1.0),
        "guess": jnp.clip(1.0 * jax.random.uniform(streams_of[1], (NT, 2, NX, COLS), jnp.float32) ** shard_levels(streams_of[1], (NT, 2, NX, COLS), ((0, 8), (2, 4)), -0.2, 0.2), 0.0, 1.0),
        "kappa": jnp.clip(jnp.exp(math.log(0.05) - 2.3025851 * jax.random.uniform(streams_of[2], (2, NX, COLS), jnp.float32) ** shard_levels(streams_of[2], (2, NX, COLS), ((1, 4),), -0.2, 0.2)), 0.005, 0.05),
        "feed": jnp.clip(jnp.exp(math.log(0.01) - 1.6094378 * jax.random.uniform(streams_of[3], (NX, COLS), jnp.float32) ** shard_levels(streams_of[3], (NX, COLS), ((0, 4),), -0.2, 0.2)), 0.002, 0.01),
        "kill": jnp.clip(jnp.exp(math.log(0.008) - 1.3862944 * jax.random.uniform(streams_of[4], (NX, COLS), jnp.float32) ** shard_levels(streams_of[4], (NX, COLS), ((0, 4),), -0.2, 0.2)), 0.002, 0.008),
        "react": jnp.clip(jnp.exp(math.log(0.008) - 1.3862944 * jax.random.uniform(streams_of[5], (NX, COLS), jnp.float32) ** shard_levels(streams_of[5], (NX, COLS), ((0, 4),), -0.2, 0.2)), 0.002, 0.008),
    }


def coarsen(field):
    shape = field.shape
    blocks = field.reshape(shape[:-2] + (shape[-2] // 2, 2, shape[-1] // 2, 2))
    return blocks.mean(axis=(-3, -1))


def refine(field):
    return jnp.repeat(jnp.repeat(field, 2, axis=-2), 2, axis=-1)


def advance(state, row_padded, coeffs):
    spread, supply, removal, coupling = coeffs
    padded = jnp.pad(row_padded, [(0, 0)] * (row_padded.ndim - 1) + [(1, 1)])
    laplace = padded[..., :-2, 1:-1] + padded[..., 2:, 1:-1] + padded[..., 1:-1, :-2] + padded[..., 1:-1, 2:] - 4.0 * state
    first_species = state[..., 0, :, :]
    second_species = state[..., 1, :, :]
    coupled = coupling * first_species * second_species * second_species
    next_first = first_species + spread[0] * laplace[..., 0, :, :] - coupled + supply * (1.0 - first_species)
    next_second = second_species + spread[1] * laplace[..., 1, :, :] + coupled - (supply + removal) * second_species
    return jnp.stack([next_first, next_second], axis=-3)


def stepping(state, coeffs):
    row_padded = jnp.pad(state, [(0, 0)] * (state.ndim - 2) + [(1, 1), (0, 0)])
    return advance(state, row_padded, coeffs)


def relax_sweep(series, opening, coeffs, forcing):
    current = jnp.concatenate([opening[None], series[:-1, SPAN - 1]])
    columns = []
    for position in range(SPAN - 1):
        current = stepping(current, coeffs)
        if forcing is not None:
            current = current + forcing[:, position]
        columns.append(current)
    columns.append(series[:, SPAN - 1])
    return jnp.stack(columns, axis=1)


def reference(initial, guess, kappa, feed, kill, react):
    level_zero = (kappa, feed, kill, react)
    spread_one = coarsen(kappa)
    supply_one = coarsen(feed)
    removal_one = coarsen(kill)
    coupling_one = coarsen(react)
    level_one = (2.0 * spread_one, 8.0 * supply_one, 8.0 * removal_one, 8.0 * coupling_one)
    level_two = (4.0 * coarsen(spread_one), 64.0 * coarsen(supply_one), 64.0 * coarsen(removal_one), 64.0 * coarsen(coupling_one))
    count_one = guess.shape[0] // SPAN
    count_two = count_one // SPAN
    series = guess.reshape((count_one, SPAN) + guess.shape[1:])
    series = relax_sweep(series, initial, level_zero, None)
    series = series.at[:, SPAN - 1].set(stepping(series[:, SPAN - 2], level_zero))
    series = relax_sweep(series, initial, level_zero, None)
    ends = series[:, SPAN - 1]
    residual = stepping(series[:, SPAN - 2], level_zero) - ends
    restricted = coarsen(ends)
    start_one = coarsen(initial)
    earlier = jnp.concatenate([start_one[None], restricted[:-1]])
    forcing_one = coarsen(residual) + restricted - stepping(earlier, level_one)
    middle = restricted.reshape((count_two, SPAN) + restricted.shape[1:])
    forcing_grid = forcing_one.reshape(middle.shape)
    middle = relax_sweep(middle, start_one, level_one, forcing_grid)
    coarse_values = coarsen(middle[:, SPAN - 1])
    predicted = stepping(middle[:, SPAN - 2], level_one) + forcing_grid[:, SPAN - 1]
    coarse_right = coarsen(predicted - middle[:, SPAN - 1]) + coarse_values
    start_two = coarsen(start_one)
    coarse_prev = jnp.concatenate([start_two[None], coarse_values[:-1]])
    forcing_two = coarse_right - stepping(coarse_prev, level_two)

    def march(previous, forcing_step):
        following = stepping(previous, level_two) + forcing_step
        return following, following

    unused, solved = lax.scan(march, start_two, forcing_two)
    middle = middle.at[:, SPAN - 1].add(refine(solved - coarse_values))
    middle = relax_sweep(middle, start_one, level_one, forcing_grid)
    series = series.at[:, SPAN - 1].add(refine(middle.reshape(restricted.shape) - restricted))
    series = relax_sweep(series, initial, level_zero, None)
    return series.reshape(guess.shape)
```

```python
import jax
import jax.numpy as jnp
from jax import lax
from jax.experimental import pallas as pl
from jax.experimental.pallas import tpu as pltpu
from jax.sharding import PartitionSpec as P

SPAN = 8
H = 8
GROUP = SPAN // 2
MESH = pl.DeviceIdType.MESH
F32 = jnp.float32


def phi(src, coef, quad, first, last, total, emit):
    cols = src.shape[-1]
    lane = lax.broadcasted_iota(jnp.int32, (8, cols), 1)
    row = lax.broadcasted_iota(jnp.int32, (8, cols), 0)
    cache = {}

    def load(b, sp):
        b = b % total
        if (b, sp) not in cache:
            x = src[sp, b * 8 : b * 8 + 8, :]
            cache[b, sp] = (x, pltpu.roll(x, 1, 0), pltpu.roll(x, 7, 0))
        return cache[b, sp]

    for blk in range(first, last):
        rows = slice(blk * 8, blk * 8 + 8)
        x = []
        around = []
        for sp in range(2):
            v, down, up = load(blk, sp)
            above = jnp.where(row == 0, load(blk - 1, sp)[1], down)
            below = jnp.where(row == 7, load(blk + 1, sp)[2], up)
            left = jnp.where(lane == 0, 0.0, pltpu.roll(v, 1, 1))
            right = jnp.where(lane == cols - 1, 0.0, pltpu.roll(v, cols - 1, 1))
            x.append(v)
            around.append((above + below) + (left + right))
        c = coef[4, rows, :] * x[0] * (x[1] * x[1])
        emit(blk, 0, quad[0, rows, :] * x[0] + coef[0, rows, :] * around[0] + (coef[2, rows, :] - c))
        emit(blk, 1, quad[1, rows, :] * x[1] + coef[1, rows, :] * around[1] + c)


def into(dst, shift=0):
    def emit(b, sp, value):
        dst[sp, b * 8 + shift : b * 8 + shift + 8, :] = value

    return emit


def pieces(x):
    t = x * 65537.0
    a = t - (t - x)
    r = x - a
    t = r * 65537.0
    b = t - (t - r)
    return [a, b, r - b]


def times(x, matrix):
    n = x.shape[0]
    y = jnp.dot(jnp.concatenate(pieces(x), 0), matrix, preferred_element_type=F32)
    return y[:n] + y[n : 2 * n] + y[2 * n :]


def row_matrix(out_rows, in_rows, shift, expand):
    i = lax.broadcasted_iota(jnp.int32, (out_rows, in_rows), 0)
    j = lax.broadcasted_iota(jnp.int32, (out_rows, in_rows), 1)
    d = (i - 2 * j if expand else j - 2 * i) + shift
    m = jnp.where((d == 0) | (d == 1), 1.0 if expand else 0.25, 0.0)
    return jnp.concatenate([m, m, m], 1)


def rows_times(matrix, x):
    return jnp.dot(matrix, jnp.concatenate(pieces(x), 0), preferred_element_type=F32)


def coarsen(xs, wide, cmat):
    rows, cols = xs[0].shape
    out_rows = (rows - 2 * H) // 2 + 2 * H if wide else rows // 2
    m = row_matrix(out_rows, rows, H if wide else 0, False)
    y = times(jnp.concatenate(xs, 0), cmat[0:cols, 0 : cols // 2])
    return [rows_times(m, y[k * rows : (k + 1) * rows]) for k in range(len(xs))]


def refine(xs, emat):
    rows, cols = xs[0].shape
    out_rows = (rows - 2 * H) * 2 + 2 * H
    m = row_matrix(out_rows, rows, H, True)
    y = jnp.concatenate([rows_times(m, x) for x in xs], 0)
    z = times(y, emat[0:cols, 0 : 2 * cols])
    return [z[k * out_rows : (k + 1) * out_rows] for k in range(len(xs))]


def kernel(
    T, S,
    initial, guess, kappa, feed, kill, react, out,
    cf, q0, c1, q1, c2, q2, ga, gb, ca, cb, cc, dd, st0, st1, outbuf,
    wa, wb, wc, gs, vs, vv, dl, ei, eo, zz, zy, cmat, emat,
    s_loc, s_cf, r_cf, s_g, r_g, s_c1, r_c1, s_ca, r_ca, s_cb, r_cb,
    s_vs, r_vs, s_gs, r_gs, s_e, r_e, s_d, r_d, s_out,
):
    t = lax.axis_index("tm")
    s = lax.axis_index("space")
    m = lax.rem(t, GROUP)
    base = t - m
    N = cf.shape[1] - 2 * H
    N1 = c1.shape[1] - 2 * H
    N2 = ei.shape[1] - 2 * H
    has = {-1: s > 0, 1: s < S - 1, 0: t >= 0}
    opening = t == 0
    sends = []

    def edge(n, ds):
        if ds == -1:
            return slice(0, H), slice(n + H, n + 2 * H)
        if ds == 1:
            return slice(n - H, n), slice(0, H)
        return slice(0, n), slice(H, n + H)

    def shift(sl, by):
        return slice(sl.start + by, sl.stop + by)

    def send(cond, src, dst, ssem, rsem, dt, ds):
        copy = pltpu.make_async_remote_copy(
            src_ref=src, dst_ref=dst, send_sem=ssem, recv_sem=rsem,
            device_id=(t + dt, s + ds), device_id_type=MESH,
        )

        @pl.when(cond)
        def _():
            copy.start()

        sends.append((cond, copy))

    def arrive(cond, dst, rsem):
        @pl.when(cond)
        def _():
            pltpu.make_async_copy(dst, dst, rsem).wait()

    mid = slice(H, N + H)
    local = [
        pltpu.make_async_copy(guess.at[SPAN - 1], gb.at[:, mid], s_loc.at[0]),
        pltpu.make_async_copy(kappa, cf.at[0:2, mid], s_loc.at[1]),
        pltpu.make_async_copy(feed, cf.at[2, mid], s_loc.at[2]),
        pltpu.make_async_copy(kill, cf.at[3, mid], s_loc.at[3]),
        pltpu.make_async_copy(react, cf.at[4, mid], s_loc.at[4]),
    ]
    for c in local:
        c.start()
    opened = [
        pltpu.make_async_copy(initial, ga.at[:, mid], s_loc.at[5]),
        pltpu.make_async_copy(initial, ca.at[:, mid], s_loc.at[6]),
    ]

    @pl.when(opening)
    def _():
        for c in opened:
            c.start()

    for ds in (-1, 1):
        @pl.when(jnp.logical_not(has[ds]))
        def _():
            for ref, n in ((cf, N), (ga, N), (gb, N), (ca, N), (cb, N), (c1, N1), (vs, N1)):
                rows = slice(0, H) if ds == -1 else slice(n + H, n + 2 * H)
                ref[:, rows, :] = jnp.zeros((ref.shape[0], H, ref.shape[2]), F32)
            rows = slice(0, H) if ds == -1 else slice(N1 + H, N1 + 2 * H)
            gs[:, :, rows, :] = jnp.zeros((SPAN, 2, H, gs.shape[3]), F32)
            dl[:, :, rows, :] = jnp.zeros((2, 2, H, dl.shape[3]), F32)
            rows = slice(0, H) if ds == -1 else slice(N2 + H, N2 + 2 * H)
            ei[:, rows, :] = jnp.zeros((2, H, ei.shape[2]), F32)

    @pl.when(base == 0)
    def _():
        ei[...] = jnp.zeros(ei.shape, F32)

    barrier = pltpu.get_barrier_semaphore()
    count = jnp.int32(0)
    for dt in range(-GROUP, GROUP + 1):
        other = t + dt
        known = (other >= 0) & (other < T)
        if abs(dt) not in (0, 1, GROUP):
            known = known & (m + dt >= 0) & (m + dt < GROUP)
        for ds in (-1, 0, 1):
            if dt == 0 and ds == 0:
                continue
            there = known & has[ds]

            @pl.when(there)
            def _():
                pl.semaphore_signal(barrier, inc=1, device_id=(other, s + ds), device_id_type=MESH)

            count = count + there.astype(jnp.int32)
    pl.semaphore_wait(barrier, count)

    further = t < T - 1
    for ds in (-1, 1):
        src, dst = edge(N, ds)
        k = (ds + 1) // 2
        send(has[ds], guess.at[SPAN - 1, :, src], gb.at[:, dst], s_cf.at[k, 4], r_cf.at[k, 4], 0, ds)
        send(has[ds], kappa.at[:, src], cf.at[0:2, dst], s_cf.at[k, 0], r_cf.at[k, 0], 0, ds)
        send(has[ds], feed.at[src], cf.at[2, dst], s_cf.at[k, 1], r_cf.at[k, 1], 0, ds)
        send(has[ds], kill.at[src], cf.at[3, dst], s_cf.at[k, 2], r_cf.at[k, 2], 0, ds)
        send(has[ds], react.at[src], cf.at[4, dst], s_cf.at[k, 3], r_cf.at[k, 3], 0, ds)
    for ds in (0, -1, 1):
        src, dst = edge(N, ds)
        k = ds + 1
        send(further & has[ds], guess.at[2 * SPAN - 1, :, src], ga.at[:, dst], s_g.at[0, k], r_g.at[k], 1, ds)
        if ds:
            send(opening & has[ds], initial.at[:, src], ga.at[:, dst], s_g.at[1, k], r_g.at[k], 0, ds)
            send(opening & has[ds], initial.at[:, src], ca.at[:, dst], s_g.at[2, k], r_ca.at[k], 0, ds)

    ii = lax.broadcasted_iota(jnp.int32, cmat.shape, 0) - 2 * lax.broadcasted_iota(jnp.int32, cmat.shape, 1)
    cmat[...] = jnp.where((ii == 0) | (ii == 1), 1.0, 0.0)
    jj = lax.broadcasted_iota(jnp.int32, emat.shape, 1) - 2 * lax.broadcasted_iota(jnp.int32, emat.shape, 0)
    emat[...] = jnp.where((jj == 0) | (jj == 1), 1.0, 0.0)
    eo[...] = jnp.zeros(eo.shape, F32)

    for c in local:
        c.wait()
    for ds in (-1, 1):
        k = (ds + 1) // 2
        dst = edge(N, ds)[1]
        arrive(has[-ds], gb.at[:, dst], r_cf.at[k, 4])
        arrive(has[-ds], cf.at[0:2, dst], r_cf.at[k, 0])
        arrive(has[-ds], cf.at[2, dst], r_cf.at[k, 1])
        arrive(has[-ds], cf.at[3, dst], r_cf.at[k, 2])
        arrive(has[-ds], cf.at[4, dst], r_cf.at[k, 3])

    def quads(coef, quad):
        quad[0] = 1.0 - coef[2] - 4.0 * coef[0]
        quad[1] = 1.0 - (coef[2] + coef[3]) - 4.0 * coef[1]

    quads(cf, q0)
    blocks = (N + 2 * H) // 8

    def interval(src, emit):
        phi(src, cf, q0, 0, blocks, blocks, into(st0))

        @pl.loop(0, 3)
        def _(_):
            phi(st0, cf, q0, 0, blocks, blocks, into(st1))
            phi(st1, cf, q0, 0, blocks, blocks, into(st0))

        phi(st0, cf, q0, 1, blocks - 1, blocks, emit)

    interval(gb, into(cc, -H))
    for ds in (0, -1, 1):
        src, dst = edge(N, ds)
        send(further & has[ds], cc.at[:, src], ca.at[:, dst], s_ca.at[ds + 1], r_ca.at[ds + 1], 1, ds)

    scale = (2.0, 2.0, 8.0, 8.0, 8.0)
    for k, x in enumerate(coarsen([cf[k, mid, :] for k in range(5)], False, cmat)):
        c1[k, H : H + N1, :] = scale[k] * x
    for ds in (-1, 1):
        src, dst = edge(N1, ds)
        k = (ds + 1) // 2
        send(has[ds], c1.at[:, shift(src, H)], c1.at[:, dst], s_c1.at[k], r_c1.at[k], 0, ds)
    for k, x in enumerate(coarsen([c1[k, H : H + N1, :] for k in range(5)], False, cmat)):
        c2[k, H : H + N2, :] = scale[k] * x
    q2[0, H : H + N2, :] = 1.0 - c2[2, H : H + N2, :] - 4.0 * c2[0, H : H + N2, :]
    q2[1, H : H + N2, :] = 1.0 - (c2[2, H : H + N2, :] + c2[3, H : H + N2, :]) - 4.0 * c2[1, H : H + N2, :]

    for c in opened:
        @pl.when(opening)
        def _():
            c.wait()
    for ds in (-1, 0, 1):
        cond = has[-ds] if ds else jnp.logical_not(opening)
        arrive(cond, ga.at[:, edge(N, ds)[1]], r_g.at[ds + 1])
    interval(ga, into(cb))
    for ds in (-1, 1):
        src, dst = edge(N, ds)
        k = (ds + 1) // 2
        send(has[ds], cb.at[:, shift(src, H)], cb.at[:, dst], s_cb.at[k], r_cb.at[k], 0, ds)
    for k, x in enumerate(coarsen([cc[0], cc[1]], False, cmat)):
        wc[k] = x
    for ds in (-1, 1):
        arrive(has[-ds], c1.at[:, edge(N1, ds)[1]], r_c1.at[(ds + 1) // 2])
    quads(c1, q1)
    blocks1 = (N1 + 2 * H) // 8

    for ds in (-1, 0, 1):
        cond = has[-ds] if ds else jnp.logical_not(opening)
        arrive(cond, ca.at[:, edge(N, ds)[1]], r_ca.at[ds + 1])
    for k, x in enumerate(coarsen([ca[0], ca[1]], True, cmat)):
        wa[k] = x
    first = m == 0

    @pl.when(first)
    def _():
        vs[:, H : H + N1, :] = wa[:, H : H + N1, :]

    for dm in range(GROUP):
        for ds in (0, -1, 1):
            if dm or ds:
                src, dst = edge(N1, ds)
                send(first & has[ds], wa.at[:, shift(src, H)], vs.at[:, dst],
                     s_vs.at[dm, ds + 1], r_vs.at[ds + 1], dm, ds)

    def forcing(which, w, start):
        interval(start, into(dd, -H))
        slot = 2 * m + which
        r = coarsen([dd[0], dd[1]], False, cmat)
        last = jnp.where(m == GROUP - 1, 1.0, 0.0) if which else None

        def emit(b, sp, value):
            rows = slice(b * 8 - H, b * 8 - H + 8)
            g = r[sp][rows] - value
            if which:
                g = g - last * wc[sp, rows, :]
            gs[slot, sp, b * 8 : b * 8 + 8, :] = g

        phi(w, c1, q1, 1, blocks1 - 1, blocks1, emit)
        for dm in range(-GROUP + 1, GROUP):
            inside = (m + dm >= 0) & (m + dm < GROUP)
            for ds in (0, -1, 1):
                if dm or ds:
                    src, dst = edge(N1, ds)
                    send(inside & has[ds], gs.at[slot, :, shift(src, H)], gs.at[slot, :, dst],
                         s_gs.at[which, dm + GROUP - 1, ds + 1], r_gs.at[slot, ds + 1], dm, ds)

    forcing(0, wa, ca)
    for ds in (-1, 1):
        arrive(has[-ds], cb.at[:, edge(N, ds)[1]], r_cb.at[(ds + 1) // 2])
    for k, x in enumerate(coarsen([cb[0], cb[1]], True, cmat)):
        wb[k] = x
    forcing(1, wb, cb)

    for ds in (0, -1, 1):
        cond = has[-ds] if ds else jnp.logical_not(first)
        arrive(cond, vs.at[:, edge(N1, ds)[1]], r_vs.at[ds + 1])
    vv[0] = vs[...]

    def middle_step(i, wait):
        if wait:
            for ds in (0, -1, 1):
                cond = has[-ds] if ds else (m != i // 2)
                arrive(cond, gs.at[i, :, edge(N1, ds)[1]], r_gs.at[i, ds + 1])

        def emit(b, sp, value):
            rows = slice(b * 8, b * 8 + 8)
            vv[i + 1, sp, rows, :] = value + gs[i, sp, rows, :]

        phi(vv.at[i], c1, q1, 0, blocks1, blocks1, emit)

    for i in range(SPAN):
        middle_step(i, True)

    r = coarsen([vv[SPAN, sp, H : H + N1, :] for sp in range(2)], False, cmat)
    z = coarsen([vs[0], vs[1]], True, cmat)
    for ds in (-1, 0, 1):
        cond = (base > 0) & has[-ds]
        arrive(cond, ei.at[:, edge(N2, ds)[1]], r_e.at[ds + 1])
    for sp in range(2):
        zz[sp] = z[sp]
        zy[sp] = z[sp] + ei[sp]
    top = (N2 + 2 * H) // 8

    def emit_old(b, sp, value):
        eo[sp, b * 8 : b * 8 + 8, :] = r[sp][b * 8 - H : b * 8 - H + 8] - value

    def emit_new(b, sp, value):
        rows = slice(b * 8, b * 8 + 8)
        eo[sp, rows, :] = eo[sp, rows, :] + value

    phi(zz, c2, q2, 1, top - 1, top, emit_old)
    phi(zy, c2, q2, 1, top - 1, top, emit_new)
    for ds in (0, -1, 1):
        src, dst = edge(N2, ds)
        send((t + GROUP < T) & has[ds], eo.at[:, shift(src, H)], ei.at[:, dst],
             s_e.at[ds + 1], r_e.at[ds + 1], GROUP, ds)

    p = refine([ei[0], ei[1]], emat)
    for sp in range(2):
        vv[0, sp] = vs[sp] + p[sp]
    for i in range(SPAN - 1):
        middle_step(i, False)
    p = refine([eo[0], eo[1]], emat)
    for sp in range(2):
        vv[SPAN, sp, H : H + N1, :] = wc[sp] + p[sp][H : H + N1]
    inner = slice(H, H + N1)
    dl[0, :, inner, :] = vv[2 * m, :, inner, :] - wa[:, inner, :]
    dl[1, :, inner, :] = vv[2 * m + 1, :, inner, :] - wb[:, inner, :]
    for ds in (-1, 1):
        src, dst = edge(N1, ds)
        k = (ds + 1) // 2
        send(has[ds], dl.at[:, :, shift(src, H)], dl.at[:, :, dst], s_d.at[k], r_d.at[k], 0, ds)

    def done(i):
        return pltpu.make_async_copy(outbuf.at[i], out.at[i], s_out.at[i])

    zeros = jnp.zeros((H, c1.shape[2]), F32)
    tail = [
        jnp.concatenate([zeros, vv[2 * m + 2, sp, inner, :] - wc[sp], zeros], 0) for sp in range(2)
    ]
    p = refine(tail, emat)
    for sp in range(2):
        outbuf[2 * SPAN - 1, sp] = cc[sp] + p[sp][mid]
    done(2 * SPAN - 1).start()

    for ds in (-1, 1):
        arrive(has[-ds], dl.at[:, :, edge(N1, ds)[1]], r_d.at[(ds + 1) // 2])
    p = refine([dl[0, 0], dl[0, 1], dl[1, 0], dl[1, 1]], emat)
    for sp in range(2):
        ga[sp] = ca[sp] + p[sp]
        u = cb[sp] + p[2 + sp]
        gb[sp] = u
        outbuf[SPAN - 1, sp] = u[mid]
    done(SPAN - 1).start()

    def final(src, at):
        def step(a, b, i):
            def emit(blk, sp, value):
                b[sp, blk * 8 : blk * 8 + 8, :] = value
                if 1 <= blk < blocks - 1:
                    outbuf[i, sp, blk * 8 - H : blk * 8 - H + 8, :] = value

            phi(a, cf, q0, 0, blocks, blocks, emit)
            done(i).start()

        step(src, st0, at)

        @pl.loop(0, 3)
        def _(k):
            step(st0, st1, at + 1 + 2 * k)
            step(st1, st0, at + 2 + 2 * k)

    final(ga, 0)
    final(gb, SPAN)
    for i in range(2 * SPAN):
        done(i).wait()
    for cond, copy in sends:
        @pl.when(cond)
        def _():
            copy.wait_send()


def local(T, S, initial, guess, kappa, feed, kill, react):
    _, N, C = initial.shape
    W, W1, W2 = N + 2 * H, N // 2 + 2 * H, N // 4 + 2 * H
    C1, C2 = C // 2, C // 4
    V = lambda *shape: pltpu.VMEM(shape, F32)
    D = lambda *shape: pltpu.SemaphoreType.DMA(shape)
    scratch = [
        V(5, W, C), V(2, W, C), V(5, W1, C1), V(2, W1, C1), V(5, W2, C2), V(2, W2, C2),
        V(2, W, C), V(2, W, C), V(2, W, C), V(2, W, C), V(2, N, C), V(2, N, C),
        V(2, W, C), V(2, W, C), V(2 * SPAN, 2, N, C),
        V(2, W1, C1), V(2, W1, C1), V(2, N // 2, C1), V(SPAN, 2, W1, C1), V(2, W1, C1),
        V(SPAN + 1, 2, W1, C1), V(2, 2, W1, C1), V(2, W2, C2), V(2, W2, C2), V(2, W2, C2), V(2, W2, C2),
        V(C, C1), V(C1, C),
        D(7), D(2, 5), D(2, 5), D(3, 3), D(3), D(2), D(2), D(3), D(3), D(2), D(2),
        D(GROUP, 3), D(3), D(2, 2 * GROUP - 1, 3), D(SPAN, 3), D(3), D(3), D(2), D(2), D(2 * SPAN),
    ]

    def body(*refs):
        kernel(T, S, *refs)

    return pl.pallas_call(
        body,
        out_shape=jax.ShapeDtypeStruct(guess.shape, F32),
        in_specs=[pl.BlockSpec(memory_space=pl.ANY)] * 6,
        out_specs=pl.BlockSpec(memory_space=pl.ANY),
        scratch_shapes=scratch,
        compiler_params=pltpu.CompilerParams(
            collective_id=0, has_side_effects=True, vmem_limit_bytes=48 * 1024 * 1024
        ),
    )(initial, guess, kappa, feed, kill, react)


def solution(mesh):
    T, S = mesh.shape["tm"], mesh.shape["space"]
    in_specs = (
        P(None, "space", None),
        P("tm", None, "space", None),
        P(None, "space", None),
        P("space", None),
        P("space", None),
        P("space", None),
    )
    out_specs = P("tm", None, "space", None)

    def run(*args):
        return local(T, S, *args)

    return jax.shard_map(run, mesh=mesh, in_specs=in_specs, out_specs=out_specs, check_vma=False)
```

```python
import jax
import jax.numpy as jnp
from jax import lax
from jax.experimental import pallas as pl
from jax.experimental.pallas import tpu as pltpu
from jax.sharding import PartitionSpec as P

SPAN = 8
H = 8
GROUP = SPAN // 2
MESH = pl.DeviceIdType.MESH
F32 = jnp.float32


def phi(src, coef, quad, first, last, total, emit):
    cols = src.shape[-1]
    lane = lax.broadcasted_iota(jnp.int32, (8, cols), 1)
    row = lax.broadcasted_iota(jnp.int32, (8, cols), 0)
    cache = {}

    def load(b, sp):
        b = b % total
        if (b, sp) not in cache:
            x = src[sp, b * 8 : b * 8 + 8, :]
            cache[b, sp] = (x, pltpu.roll(x, 1, 0), pltpu.roll(x, 7, 0))
        return cache[b, sp]

    for blk in range(first, last):
        rows = slice(blk * 8, blk * 8 + 8)
        x = []
        around = []
        for sp in range(2):
            v, down, up = load(blk, sp)
            above = jnp.where(row == 0, load(blk - 1, sp)[1], down)
            below = jnp.where(row == 7, load(blk + 1, sp)[2], up)
            left = jnp.where(lane == 0, 0.0, pltpu.roll(v, 1, 1))
            right = jnp.where(lane == cols - 1, 0.0, pltpu.roll(v, cols - 1, 1))
            x.append(v)
            around.append((above + below) + (left + right))
        c = coef[4, rows, :] * x[0] * (x[1] * x[1])
        emit(blk, 0, quad[0, rows, :] * x[0] + coef[0, rows, :] * around[0] + (coef[2, rows, :] - c))
        emit(blk, 1, quad[1, rows, :] * x[1] + coef[1, rows, :] * around[1] + c)


def into(dst, shift=0):
    def emit(b, sp, value):
        dst[sp, b * 8 + shift : b * 8 + shift + 8, :] = value

    return emit


def pieces(x):
    t = x * 65537.0
    a = t - (t - x)
    r = x - a
    t = r * 65537.0
    b = t - (t - r)
    return [a, b, r - b]


def times(x, matrix):
    n = x.shape[0]
    y = jnp.dot(jnp.concatenate(pieces(x), 0), matrix, preferred_element_type=F32)
    return y[:n] + y[n : 2 * n] + y[2 * n :]


def row_matrix(out_rows, in_rows, shift, expand):
    i = lax.broadcasted_iota(jnp.int32, (out_rows, in_rows), 0)
    j = lax.broadcasted_iota(jnp.int32, (out_rows, in_rows), 1)
    d = (i - 2 * j if expand else j - 2 * i) + shift
    m = jnp.where((d == 0) | (d == 1), 1.0 if expand else 0.25, 0.0)
    return jnp.concatenate([m, m, m], 1)


def rows_times(matrix, x):
    return jnp.dot(matrix, jnp.concatenate(pieces(x), 0), preferred_element_type=F32)


def coarsen(xs, wide, cmat):
    rows, cols = xs[0].shape
    out_rows = (rows - 2 * H) // 2 + 2 * H if wide else rows // 2
    m = row_matrix(out_rows, rows, H if wide else 0, False)
    y = times(jnp.concatenate(xs, 0), cmat[0:cols, 0 : cols // 2])
    return [rows_times(m, y[k * rows : (k + 1) * rows]) for k in range(len(xs))]


def refine(xs, emat):
    rows, cols = xs[0].shape
    out_rows = (rows - 2 * H) * 2 + 2 * H
    m = row_matrix(out_rows, rows, H, True)
    y = jnp.concatenate([rows_times(m, x) for x in xs], 0)
    z = times(y, emat[0:cols, 0 : 2 * cols])
    return [z[k * out_rows : (k + 1) * out_rows] for k in range(len(xs))]


def kernel(
    T, S,
    initial, guess, kappa, feed, kill, react, out,
    cf, q0, c1, q1, c2, q2, ga, gb, ca, cb, cc, st0, st1, outbuf,
    wa, wb, wc, gs, vs, vv, ps, pr, ei, eo, zz, zy, cmat, emat,
    s_loc, r_cf, r_gb, r_ga, r_c1, r_ca, r_cb, r_vs, r_gs, r_fw, r_e, r_d, s_out, s_send,
):
    t = lax.axis_index("tm")
    s = lax.axis_index("space")
    m = lax.rem(t, GROUP)
    base = t - m
    N = cf.shape[1] - 2 * H
    N1 = c1.shape[1] - 2 * H
    N2 = ei.shape[1] - 2 * H
    has = {-1: s > 0, 1: s < S - 1}
    opening = t == 0
    further = t < T - 1
    first = m == 0
    follows = base > 0
    leads = t + GROUP < T
    partner = m + 1 - 2 * lax.rem(m, 2)
    across = lax.rem(m + 2, GROUP)
    sends = []
    number = [0]

    def edge(n, ds):
        if ds == -1:
            return slice(0, H), slice(n + H, n + 2 * H)
        if ds == 1:
            return slice(n - H, n), slice(0, H)
        return slice(0, n), slice(H, n + H)

    def shift(sl, by):
        return slice(sl.start + by, sl.stop + by)

    def begin(cond, copies):
        made = []
        for src, dst, rsem, tt, ss in copies:
            made.append(pltpu.make_async_remote_copy(
                src_ref=src, dst_ref=dst, send_sem=s_send.at[number[0]], recv_sem=rsem,
                device_id=(tt, ss), device_id_type=MESH,
            ))
            number[0] += 1

        def go():
            for c in made:
                c.start()

        if cond is None:
            go()
        else:
            pl.when(cond)(go)
        sends.append((cond, made))

    def arrive(cond, waits):
        def go():
            for dst, rsem in waits:
                pltpu.make_async_copy(dst, dst, rsem).wait()

        if cond is None:
            go()
        else:
            pl.when(cond)(go)

    mid = slice(H, N + H)
    inner = slice(H, N1 + H)
    core = slice(H, N2 + H)
    local = [
        pltpu.make_async_copy(guess.at[SPAN - 1], gb.at[:, mid], s_loc.at[0]),
        pltpu.make_async_copy(kappa, cf.at[0:2, mid], s_loc.at[1]),
        pltpu.make_async_copy(feed, cf.at[2, mid], s_loc.at[2]),
        pltpu.make_async_copy(kill, cf.at[3, mid], s_loc.at[3]),
        pltpu.make_async_copy(react, cf.at[4, mid], s_loc.at[4]),
    ]
    for c in local:
        c.start()
    opened = [
        pltpu.make_async_copy(initial, ga.at[:, mid], s_loc.at[5]),
        pltpu.make_async_copy(initial, ca.at[:, mid], s_loc.at[6]),
    ]

    @pl.when(opening)
    def _():
        for c in opened:
            c.start()

    for ds in (-1, 1):
        @pl.when(jnp.logical_not(has[ds]))
        def _():
            for ref, n in ((cf, N), (ga, N), (gb, N), (ca, N), (cb, N), (c1, N1), (vs, N1)):
                rows = slice(0, H) if ds == -1 else slice(n + H, n + 2 * H)
                ref[:, rows, :] = jnp.zeros((ref.shape[0], H, ref.shape[2]), F32)
            rows = slice(0, H) if ds == -1 else slice(N1 + H, N1 + 2 * H)
            gs[:, :, rows, :] = jnp.zeros((SPAN, 2, H, gs.shape[3]), F32)
            pr[(1 - ds) // 2] = jnp.zeros(pr.shape[1:], F32)
            rows = slice(0, H) if ds == -1 else slice(N2 + H, N2 + 2 * H)
            ei[:, rows, :] = jnp.zeros((2, H, ei.shape[2]), F32)

    @pl.when(base == 0)
    def _():
        ei[...] = jnp.zeros(ei.shape, F32)

    barrier = pltpu.get_barrier_semaphore()
    count = jnp.int32(0)
    known = []
    for dt in (-GROUP, -1, 0, 1, GROUP):
        known.append((t + dt, (t + dt >= 0) & (t + dt < T), dt == 0))
    known.append((base + across, t >= 0, False))
    far = GROUP - 1 - m
    known.append((base + far, (m == 0) | (m == GROUP - 1), False))
    for other, there, own in known:
        for ds in (-1, 0, 1):
            if own and ds == 0:
                continue
            cond = there & has[ds] if ds else there

            @pl.when(cond)
            def _():
                pl.semaphore_signal(barrier, inc=1, device_id=(other, s + ds), device_id_type=MESH)

            count = count + cond.astype(jnp.int32)

    pl.semaphore_wait(barrier, count)

    for ds in (-1, 1):
        src, dst = edge(N, ds)
        k = (ds + 1) // 2
        begin(has[ds], [
            (guess.at[SPAN - 1, :, src], gb.at[:, dst], r_gb.at[k], t, s + ds),
            (kappa.at[:, src], cf.at[0:2, dst], r_cf.at[k, 0], t, s + ds),
            (feed.at[src], cf.at[2, dst], r_cf.at[k, 1], t, s + ds),
            (kill.at[src], cf.at[3, dst], r_cf.at[k, 2], t, s + ds),
            (react.at[src], cf.at[4, dst], r_cf.at[k, 3], t, s + ds),
        ])
    begin(further, [(guess.at[2 * SPAN - 1], ga.at[:, mid], r_ga.at[1], t + 1, s)])

    ii = lax.broadcasted_iota(jnp.int32, cmat.shape, 0) - 2 * lax.broadcasted_iota(jnp.int32, cmat.shape, 1)
    cmat[...] = jnp.where((ii == 0) | (ii == 1), 1.0, 0.0)
    jj = lax.broadcasted_iota(jnp.int32, emat.shape, 1) - 2 * lax.broadcasted_iota(jnp.int32, emat.shape, 0)
    emat[...] = jnp.where((jj == 0) | (jj == 1), 1.0, 0.0)
    eo[...] = jnp.zeros(eo.shape, F32)

    for c in local:
        c.wait()
    scale = (2.0, 2.0, 8.0, 8.0, 8.0)
    for k, x in enumerate(coarsen([cf[k, mid, :] for k in range(5)], False, cmat)):
        c1[k, inner, :] = scale[k] * x
    for k, x in enumerate(coarsen([c1[k, inner, :] for k in range(5)], False, cmat)):
        c2[k, core, :] = scale[k] * x
    q2[0, core, :] = 1.0 - c2[2, core, :] - 4.0 * c2[0, core, :]
    q2[1, core, :] = 1.0 - (c2[2, core, :] + c2[3, core, :]) - 4.0 * c2[1, core, :]

    for ds in (-1, 1):
        k = (ds + 1) // 2
        dst = edge(N, ds)[1]
        arrive(has[-ds], [
            (gb.at[:, dst], r_gb.at[k]),
            (cf.at[0:2, dst], r_cf.at[k, 0]),
            (cf.at[2, dst], r_cf.at[k, 1]),
            (cf.at[3, dst], r_cf.at[k, 2]),
            (cf.at[4, dst], r_cf.at[k, 3]),
        ])
    for ds in (-1, 1):
        src, dst = edge(N, ds)
        src1, dst1 = edge(N1, ds)
        begin(further & has[ds], [
            (guess.at[2 * SPAN - 1, :, src], ga.at[:, dst], r_ga.at[ds + 1], t + 1, s + ds),
        ])
        begin(opening & has[ds], [
            (initial.at[:, src], ga.at[:, dst], r_ga.at[ds + 1], t, s + ds),
            (initial.at[:, src], ca.at[:, dst], r_ca.at[ds + 1], t, s + ds),
        ])
        begin(has[ds], [
            (c1.at[:, shift(src1, H)], c1.at[:, dst1], r_c1.at[(ds + 1) // 2], t, s + ds),
        ])

    def quads(coef, quad):
        quad[0] = 1.0 - coef[2] - 4.0 * coef[0]
        quad[1] = 1.0 - (coef[2] + coef[3]) - 4.0 * coef[1]

    quads(cf, q0)
    blocks = (N + 2 * H) // 8

    def interval(src):
        st1[...] = src[...]

        @pl.loop(0, SPAN // 2)
        def _(_):
            phi(st1, cf, q0, 0, blocks, blocks, into(st0))
            phi(st0, cf, q0, 0, blocks, blocks, into(st1))

    interval(gb)
    cc[...] = st1[:, mid, :]
    begin(further, [(cc, ca.at[:, mid], r_ca.at[1], t + 1, s)])
    for ds in (-1, 1):
        src, dst = edge(N, ds)
        begin(further & has[ds], [(cc.at[:, src], ca.at[:, dst], r_ca.at[ds + 1], t + 1, s + ds)])

    @pl.when(opening)
    def _():
        for c in opened:
            c.wait()

    arrive(jnp.logical_not(opening), [(ga.at[:, mid], r_ga.at[1])])
    for ds in (-1, 1):
        arrive(has[-ds], [(ga.at[:, edge(N, ds)[1]], r_ga.at[ds + 1])])
    interval(ga)
    cb[:, mid, :] = st1[:, mid, :]
    for ds in (-1, 1):
        src, dst = edge(N, ds)
        begin(has[ds], [(cb.at[:, shift(src, H)], cb.at[:, dst], r_cb.at[(ds + 1) // 2], t, s + ds)])

    arrive(jnp.logical_not(opening), [(ca.at[:, mid], r_ca.at[1])])
    for ds in (-1, 1):
        arrive(has[-ds], [
            (ca.at[:, edge(N, ds)[1]], r_ca.at[ds + 1]),
            (c1.at[:, edge(N1, ds)[1]], r_c1.at[(ds + 1) // 2]),
        ])
    quads(c1, q1)
    blocks1 = (N1 + 2 * H) // 8
    for k, x in enumerate(coarsen([ca[0], ca[1]], True, cmat)):
        wa[k] = x

    @pl.when(first)
    def _():
        vs[:, inner, :] = wa[:, inner, :]

    begin(first, [(wa.at[:, inner], vs.at[:, inner], r_vs.at[1], base + r, s) for r in range(1, GROUP)])
    for ds in (-1, 1):
        src, dst = edge(N1, ds)
        begin(first & has[ds], [
            (wa.at[:, shift(src, H)], vs.at[:, dst], r_vs.at[ds + 1], base + r, s + ds) for r in range(GROUP)
        ])

    def forcing(which, w, r):
        slot = 2 * m + which
        last = jnp.where(m == GROUP - 1, 1.0, 0.0) if which else None

        def emit(b, sp, value):
            rows = slice(b * 8 - H, b * 8 - H + 8)
            g = r[sp][rows] - value
            if which:
                g = g - last * wc[sp, rows, :]
            gs[slot, sp, b * 8 : b * 8 + 8, :] = g

        phi(w, c1, q1, 1, blocks1 - 1, blocks1, emit)
        begin(None, [
            (gs.at[slot, :, inner], gs.at[slot, :, inner], r_gs.at[slot, 1], base + to, s)
            for to in (across, partner)
        ])
        for ds in (-1, 1):
            src, dst = edge(N1, ds)
            begin(has[ds], [
                (gs.at[slot, :, shift(src, H)], gs.at[slot, :, dst], r_gs.at[slot, ds + 1], base + to, s + ds)
                for to in (across, partner, m)
            ])

    interval(ca)
    forcing(0, wa, coarsen([st1[0, mid, :], st1[1, mid, :]], False, cmat))
    for k, x in enumerate(coarsen([cc[0], cc[1]], False, cmat)):
        wc[k] = x
    for ds in (-1, 1):
        arrive(has[-ds], [(cb.at[:, edge(N, ds)[1]], r_cb.at[(ds + 1) // 2])])
    for k, x in enumerate(coarsen([cb[0], cb[1]], True, cmat)):
        wb[k] = x
    interval(cb)
    forcing(1, wb, coarsen([st1[0, mid, :], st1[1, mid, :]], False, cmat))

    for which in range(2):
        slot = 2 * across + which
        arrive(None, [(gs.at[slot, :, inner], r_gs.at[slot, 1])])
        for ds in (-1, 1):
            arrive(has[-ds], [(gs.at[slot, :, edge(N1, ds)[1]], r_gs.at[slot, ds + 1])])
        begin(None, [(gs.at[slot], gs.at[slot], r_fw.at[slot], base + partner, s)])

    arrive(jnp.logical_not(first), [(vs.at[:, inner], r_vs.at[1])])
    for ds in (-1, 1):
        arrive(has[-ds], [(vs.at[:, edge(N1, ds)[1]], r_vs.at[ds + 1])])
    vv[0] = vs[...]
    for sp, x in enumerate(coarsen([vs[0], vs[1]], True, cmat)):
        zz[sp] = x
    top = (N2 + 2 * H) // 8

    def emit_old(b, sp, value):
        eo[sp, b * 8 : b * 8 + 8, :] = -value

    def emit_new(b, sp, value):
        rows = slice(b * 8, b * 8 + 8)
        eo[sp, rows, :] = eo[sp, rows, :] + value

    phi(zz, c2, q2, 1, top - 1, top, emit_old)

    for which in range(2):
        slot = 2 * partner + which
        arrive(None, [(gs.at[slot, :, inner], r_gs.at[slot, 1])])
        for ds in (-1, 1):
            arrive(has[-ds], [
                (gs.at[slot, :, edge(N1, ds)[1]], r_gs.at[slot, ds + 1]),
                (gs.at[2 * m + which, :, edge(N1, ds)[1]], r_gs.at[2 * m + which, ds + 1]),
            ])
    other = lax.rem(partner + 2, GROUP)
    for which in range(2):
        slot = 2 * other + which
        arrive(None, [(gs.at[slot], r_fw.at[slot])])

    def sweep(count):
        @pl.loop(0, count)
        def _(i):
            def emit(b, sp, value):
                rows = slice(b * 8, b * 8 + 8)
                vv[i + 1, sp, rows, :] = value + gs[i, sp, rows, :]

            phi(vv.at[i], c1, q1, 0, blocks1, blocks1, emit)

    sweep(SPAN)

    r = coarsen([vv[SPAN, sp, inner, :] for sp in range(2)], False, cmat)
    arrive(follows, [(ei.at[:, core], r_e.at[1])])
    for ds in (-1, 1):
        arrive(follows & has[-ds], [(ei.at[:, edge(N2, ds)[1]], r_e.at[ds + 1])])
    for sp in range(2):
        zy[sp] = zz[sp] + ei[sp]
    phi(zy, c2, q2, 1, top - 1, top, emit_new)
    for sp in range(2):
        eo[sp, core, :] = eo[sp, core, :] + r[sp]
    begin(leads, [(eo.at[:, core], ei.at[:, core], r_e.at[1], t + GROUP, s)])
    for ds in (-1, 1):
        src, dst = edge(N2, ds)
        begin(leads & has[ds], [
            (eo.at[:, shift(src, H)], ei.at[:, dst], r_e.at[ds + 1], t + GROUP, s + ds),
        ])

    p = refine([ei[0], ei[1]], emat)
    for sp in range(2):
        vv[0, sp] = vs[sp] + p[sp]
    sweep(SPAN - 1)
    da = vv[2 * m, :, inner, :] - wa[:, inner, :]
    db = vv[2 * m + 1, :, inner, :] - wb[:, inner, :]
    half = H // 2
    for sp in range(2):
        ps[0, sp] = jnp.concatenate([da[sp, 0:half], db[sp, 0:half]], 0)
        ps[1, sp] = jnp.concatenate([da[sp, N1 - half :], db[sp, N1 - half :]], 0)
    for ds in (-1, 1):
        k = (ds + 1) // 2
        begin(has[ds], [(ps.at[k], pr.at[k], r_d.at[k], t, s + ds)])

    def done(i):
        return pltpu.make_async_copy(outbuf.at[i], out.at[i], s_out.at[i])

    p = refine([eo[0], eo[1]], emat)
    for sp in range(2):
        vv[SPAN, sp, inner, :] = wc[sp] + p[sp][inner]
    zeros = jnp.zeros((H, c1.shape[2]), F32)
    tail = [
        jnp.concatenate([zeros, vv[2 * m + 2, sp, inner, :] - wc[sp], zeros], 0) for sp in range(2)
    ]
    p = refine(tail, emat)
    for sp in range(2):
        outbuf[2 * SPAN - 1, sp] = cc[sp] + p[sp][mid]
    done(2 * SPAN - 1).start()

    for ds in (-1, 1):
        k = (ds + 1) // 2
        arrive(has[-ds], [(pr.at[k], r_d.at[k])])
    zeros = jnp.zeros((half, c1.shape[2]), F32)
    delta = []
    for which, d in enumerate((da, db)):
        rows = slice(which * half, which * half + half)
        for sp in range(2):
            delta.append(jnp.concatenate([zeros, pr[1, sp, rows, :], d[sp], pr[0, sp, rows, :], zeros], 0))
    p = refine(delta, emat)
    for sp in range(2):
        st1[sp] = ca[sp] + p[sp]
        u = cb[sp] + p[2 + sp]
        gb[sp] = u
        outbuf[SPAN - 1, sp] = u[mid]
    done(SPAN - 1).start()

    def final(at):
        def step(a, b, i):
            def emit(blk, sp, value):
                b[sp, blk * 8 : blk * 8 + 8, :] = value
                if 1 <= blk < blocks - 1:
                    outbuf[i, sp, blk * 8 - H : blk * 8 - H + 8, :] = value

            phi(a, cf, q0, 0, blocks, blocks, emit)
            done(i).start()

        @pl.loop(0, 3)
        def _(k):
            step(st1, st0, at + 2 * k)
            step(st0, st1, at + 1 + 2 * k)

        step(st1, st0, at + 6)

    final(0)
    st1[...] = gb[...]
    final(SPAN)
    for i in range(2 * SPAN):
        done(i).wait()
    for cond, made in sends:
        def settle():
            for c in made:
                c.wait_send()

        if cond is None:
            settle()
        else:
            pl.when(cond)(settle)


def local(T, S, initial, guess, kappa, feed, kill, react):
    _, N, C = initial.shape
    W, W1, W2 = N + 2 * H, N // 2 + 2 * H, N // 4 + 2 * H
    C1, C2 = C // 2, C // 4
    V = lambda *shape: pltpu.VMEM(shape, F32)
    D = lambda *shape: pltpu.SemaphoreType.DMA(shape)
    scratch = [
        V(5, W, C), V(2, W, C), V(5, W1, C1), V(2, W1, C1), V(5, W2, C2), V(2, W2, C2),
        V(2, W, C), V(2, W, C), V(2, W, C), V(2, W, C), V(2, N, C),
        V(2, W, C), V(2, W, C), V(2 * SPAN, 2, N, C),
        V(2, W1, C1), V(2, W1, C1), V(2, N // 2, C1), V(SPAN, 2, W1, C1), V(2, W1, C1),
        V(SPAN + 1, 2, W1, C1), V(2, 2, H, C1), V(2, 2, H, C1), V(2, W2, C2), V(2, W2, C2),
        V(2, W2, C2), V(2, W2, C2), V(C, C1), V(C1, C),
        D(7), D(2, 4), D(2), D(3), D(2), D(3), D(2), D(3), D(SPAN, 3), D(SPAN), D(3), D(2),
        D(2 * SPAN), D(96),
    ]

    def body(*refs):
        kernel(T, S, *refs)

    return pl.pallas_call(
        body,
        out_shape=jax.ShapeDtypeStruct(guess.shape, F32),
        in_specs=[pl.BlockSpec(memory_space=pl.ANY)] * 6,
        out_specs=pl.BlockSpec(memory_space=pl.ANY),
        scratch_shapes=scratch,
        compiler_params=pltpu.CompilerParams(
            collective_id=0, has_side_effects=True, vmem_limit_bytes=64 * 1024 * 1024
        ),
    )(initial, guess, kappa, feed, kill, react)


def solution(mesh):
    T, S = mesh.shape["tm"], mesh.shape["space"]
    in_specs = (
        P(None, "space", None),
        P("tm", None, "space", None),
        P(None, "space", None),
        P("space", None),
        P("space", None),
        P("space", None),
    )
    out_specs = P("tm", None, "space", None)

    def run(*args):
        return local(T, S, *args)

    return jax.shard_map(run, mesh=mesh, in_specs=in_specs, out_specs=out_specs, check_vma=False)
```

```python
import jax
import jax.numpy as jnp
from jax import lax
from jax.experimental import pallas as pl
from jax.experimental.pallas import tpu as pltpu
from jax.sharding import PartitionSpec as P

SPAN = 8
H = 8
GROUP = SPAN // 2
MESH = pl.DeviceIdType.MESH
F32 = jnp.float32
BF16 = jnp.bfloat16
L = 128


def phi(jobs, coef, quad, first, last, total):
    tiles = jobs[0][0].shape[-1] // L
    lane = lax.broadcasted_iota(jnp.int32, (8, L), 1)
    row = lax.broadcasted_iota(jnp.int32, (8, L), 0)
    low, high = lane == 0, lane == L - 1
    top, bottom = row == 0, row == 7
    cache = {}

    def load(job, b, sp, c):
        key = (job, b, sp, c)
        if key not in cache:
            x = jobs[job][0][sp, b * 8 : b * 8 + 8, c * L : c * L + L]
            cache[key] = (x, pltpu.roll(x, 1, 0), pltpu.roll(x, 7, 0), pltpu.roll(x, 1, 1), pltpu.roll(x, L - 1, 1))
        return cache[key]

    for blk in range(first, last):
        rows = slice(blk * 8, blk * 8 + 8)
        for c in range(tiles):
            cols = slice(c * L, c * L + L)
            k = [coef[i, rows, cols] for i in (0, 1, 2, 4)]
            q = [quad[i, rows, cols] for i in (0, 1)]
            for job, (_, emit) in enumerate(jobs):
                x, around = [], []
                for sp in range(2):
                    v, above, below, left, right = load(job, blk, sp, c)
                    if blk > 0:
                        above = jnp.where(top, load(job, blk - 1, sp, c)[1], above)
                    if blk < total - 1:
                        below = jnp.where(bottom, load(job, blk + 1, sp, c)[2], below)
                    left = jnp.where(low, load(job, blk, sp, c - 1)[3] if c > 0 else 0.0, left)
                    right = jnp.where(high, load(job, blk, sp, c + 1)[4] if c < tiles - 1 else 0.0, right)
                    x.append(v)
                    around.append((above + below) + (left + right))
                r = k[3] * x[0] * (x[1] * x[1])
                emit(0, rows, cols, q[0] * x[0] + k[0] * around[0] + (k[2] - r))
                emit(1, rows, cols, q[1] * x[1] + k[1] * around[1] + r)


def into(dst):
    def emit(sp, rows, cols, value):
        dst[sp, rows, cols] = value

    return emit


def times(x, matrix):
    n = x.shape[0]
    a = x.astype(BF16)
    r = x - a.astype(F32)
    b = r.astype(BF16)
    c = (r - b.astype(F32)).astype(BF16)
    y = jnp.dot(jnp.concatenate([a, b, c], 0), matrix, preferred_element_type=F32)
    return y[:n] + y[n : 2 * n] + y[2 * n :]


def coarsen(xs, wide, cmat, scr):
    rows, cols = xs[0].shape
    pad = H if wide else 0
    span = rows + 2 * pad
    y = times(jnp.concatenate(xs, 0), cmat[0:cols, 0 : cols // 2])
    tiles = cols // 2 // L
    for k in range(len(xs)):
        for c in range(tiles):
            at = k * span + pad
            scr[c, at : at + rows, :] = y[k * rows : (k + 1) * rows, c * L : c * L + L]
            if pad:
                scr[c, at - pad : at, :] = jnp.zeros((pad, L), F32)
                scr[c, at + rows : at + rows + pad, :] = jnp.zeros((pad, L), F32)
    out = []
    for k in range(len(xs)):
        parts = [
            scr[c, pl.ds(k * span, span // 2, stride=2), :] + scr[c, pl.ds(k * span + 1, span // 2, stride=2), :]
            for c in range(tiles)
        ]
        out.append(0.25 * (jnp.concatenate(parts, 1) if tiles > 1 else parts[0]))
    return out


def refine(xs, emat, scr):
    rows, cols = xs[0].shape
    tiles = cols // L
    span = 2 * rows
    for k, x in enumerate(xs):
        for c in range(tiles):
            for d in range(2):
                scr[c, pl.ds(k * span + d, rows, stride=2), :] = x[:, c * L : c * L + L]
    ys = []
    for k in range(len(xs)):
        parts = [scr[c, k * span + H : (k + 1) * span - H, :] for c in range(tiles)]
        ys.append(jnp.concatenate(parts, 1) if tiles > 1 else parts[0])
    z = times(jnp.concatenate(ys, 0), emat[0:cols, 0 : 2 * cols])
    n = span - 2 * H
    return [z[k * n : (k + 1) * n] for k in range(len(xs))]


def kernel(
    T, S,
    initial, guess, kappa, feed, kill, react, out,
    cf, q0, c1, q1, c2, q2, ga, gb, ca, cb, cc, st0, st1, outbuf,
    wa, wb, wc, gs, vs, vv, ps, pr, ei, eo, zz, zy, cmat, emat, scr,
    s_loc, r_cf, r_gb, r_ga, r_c1, r_ca, r_cb, r_vs, r_gs, r_fw, r_e, r_d, s_out, s_send,
):
    t = lax.axis_index("tm")
    s = lax.axis_index("space")
    m = lax.rem(t, GROUP)
    base = t - m
    N = cf.shape[1] - 2 * H
    N1 = c1.shape[1] - 2 * H
    N2 = ei.shape[1] - 2 * H
    has = {-1: s > 0, 1: s < S - 1}
    opening = t == 0
    further = t < T - 1
    first = m == 0
    follows = base > 0
    leads = t + GROUP < T
    partner = m + 1 - 2 * lax.rem(m, 2)
    across = lax.rem(m + 2, GROUP)
    sends = []
    number = [0]

    def edge(n, ds):
        if ds == -1:
            return slice(0, H), slice(n + H, n + 2 * H)
        if ds == 1:
            return slice(n - H, n), slice(0, H)
        return slice(0, n), slice(H, n + H)

    def shift(sl, by):
        return slice(sl.start + by, sl.stop + by)

    def begin(cond, copies):
        made = []
        for src, dst, rsem, tt, ss in copies:
            made.append(pltpu.make_async_remote_copy(
                src_ref=src, dst_ref=dst, send_sem=s_send.at[number[0]], recv_sem=rsem,
                device_id=(tt, ss), device_id_type=MESH,
            ))
            number[0] += 1

        def go():
            for c in made:
                c.start()

        if cond is None:
            go()
        else:
            pl.when(cond)(go)
        sends.append((cond, made))

    def arrive(cond, waits):
        def go():
            for dst, rsem in waits:
                pltpu.make_async_copy(dst, dst, rsem).wait()

        if cond is None:
            go()
        else:
            pl.when(cond)(go)

    mid = slice(H, N + H)
    inner = slice(H, N1 + H)
    core = slice(H, N2 + H)
    local = [
        pltpu.make_async_copy(guess.at[SPAN - 1], gb.at[:, mid], s_loc.at[0]),
        pltpu.make_async_copy(kappa, cf.at[0:2, mid], s_loc.at[1]),
        pltpu.make_async_copy(feed, cf.at[2, mid], s_loc.at[2]),
        pltpu.make_async_copy(kill, cf.at[3, mid], s_loc.at[3]),
        pltpu.make_async_copy(react, cf.at[4, mid], s_loc.at[4]),
    ]
    for c in local:
        c.start()
    opened = [
        pltpu.make_async_copy(initial, ga.at[:, mid], s_loc.at[5]),
        pltpu.make_async_copy(initial, ca.at[:, mid], s_loc.at[6]),
    ]

    @pl.when(opening)
    def _():
        for c in opened:
            c.start()

    for ds in (-1, 1):
        @pl.when(jnp.logical_not(has[ds]))
        def _():
            for ref, n in ((cf, N), (ga, N), (gb, N), (ca, N), (cb, N), (c1, N1), (vs, N1)):
                rows = slice(0, H) if ds == -1 else slice(n + H, n + 2 * H)
                ref[:, rows, :] = jnp.zeros((ref.shape[0], H, ref.shape[2]), F32)
            rows = slice(0, H) if ds == -1 else slice(N1 + H, N1 + 2 * H)
            gs[:, :, rows, :] = jnp.zeros((SPAN, 2, H, gs.shape[3]), F32)
            pr[(1 - ds) // 2] = jnp.zeros(pr.shape[1:], F32)
            rows = slice(0, H) if ds == -1 else slice(N2 + H, N2 + 2 * H)
            ei[:, rows, :] = jnp.zeros((2, H, ei.shape[2]), F32)

    @pl.when(base == 0)
    def _():
        ei[...] = jnp.zeros(ei.shape, F32)

    barrier = pltpu.get_barrier_semaphore()
    count = jnp.int32(0)
    known = []
    for dt in (-GROUP, -1, 0, 1, GROUP):
        known.append((t + dt, (t + dt >= 0) & (t + dt < T), dt == 0))
    known.append((base + across, t >= 0, False))
    far = GROUP - 1 - m
    known.append((base + far, (m == 0) | (m == GROUP - 1), False))
    for other, there, own in known:
        for ds in (-1, 0, 1):
            if own and ds == 0:
                continue
            cond = there & has[ds] if ds else there

            @pl.when(cond)
            def _():
                pl.semaphore_signal(barrier, inc=1, device_id=(other, s + ds), device_id_type=MESH)

            count = count + cond.astype(jnp.int32)

    pl.semaphore_wait(barrier, count)

    for ds in (-1, 1):
        src, dst = edge(N, ds)
        k = (ds + 1) // 2
        begin(has[ds], [
            (guess.at[SPAN - 1, :, src], gb.at[:, dst], r_gb.at[k], t, s + ds),
            (kappa.at[:, src], cf.at[0:2, dst], r_cf.at[k, 0], t, s + ds),
            (feed.at[src], cf.at[2, dst], r_cf.at[k, 1], t, s + ds),
            (kill.at[src], cf.at[3, dst], r_cf.at[k, 2], t, s + ds),
            (react.at[src], cf.at[4, dst], r_cf.at[k, 3], t, s + ds),
        ])
    begin(further, [(guess.at[2 * SPAN - 1], ga.at[:, mid], r_ga.at[1], t + 1, s)])

    ii = lax.broadcasted_iota(jnp.int32, cmat.shape, 0) - 2 * lax.broadcasted_iota(jnp.int32, cmat.shape, 1)
    cmat[...] = jnp.where((ii == 0) | (ii == 1), 1.0, 0.0).astype(BF16)
    jj = lax.broadcasted_iota(jnp.int32, emat.shape, 1) - 2 * lax.broadcasted_iota(jnp.int32, emat.shape, 0)
    emat[...] = jnp.where((jj == 0) | (jj == 1), 1.0, 0.0).astype(BF16)
    eo[...] = jnp.zeros(eo.shape, F32)

    for c in local:
        c.wait()
    scale = (2.0, 2.0, 8.0, 8.0, 8.0)
    for k, x in enumerate(coarsen([cf[k, mid, :] for k in range(5)], False, cmat, scr)):
        c1[k, inner, :] = scale[k] * x
    for k, x in enumerate(coarsen([c1[k, inner, :] for k in range(5)], False, cmat, scr)):
        c2[k, core, :] = scale[k] * x
    q2[0, core, :] = 1.0 - c2[2, core, :] - 4.0 * c2[0, core, :]
    q2[1, core, :] = 1.0 - (c2[2, core, :] + c2[3, core, :]) - 4.0 * c2[1, core, :]

    for ds in (-1, 1):
        k = (ds + 1) // 2
        dst = edge(N, ds)[1]
        arrive(has[-ds], [
            (gb.at[:, dst], r_gb.at[k]),
            (cf.at[0:2, dst], r_cf.at[k, 0]),
            (cf.at[2, dst], r_cf.at[k, 1]),
            (cf.at[3, dst], r_cf.at[k, 2]),
            (cf.at[4, dst], r_cf.at[k, 3]),
        ])
    for ds in (-1, 1):
        src, dst = edge(N, ds)
        src1, dst1 = edge(N1, ds)
        begin(further & has[ds], [
            (guess.at[2 * SPAN - 1, :, src], ga.at[:, dst], r_ga.at[ds + 1], t + 1, s + ds),
        ])
        begin(opening & has[ds], [
            (initial.at[:, src], ga.at[:, dst], r_ga.at[ds + 1], t, s + ds),
            (initial.at[:, src], ca.at[:, dst], r_ca.at[ds + 1], t, s + ds),
        ])
        begin(has[ds], [
            (c1.at[:, shift(src1, H)], c1.at[:, dst1], r_c1.at[(ds + 1) // 2], t, s + ds),
        ])

    def quads(coef, quad):
        quad[0] = 1.0 - coef[2] - 4.0 * coef[0]
        quad[1] = 1.0 - (coef[2] + coef[3]) - 4.0 * coef[1]

    quads(cf, q0)
    blocks = (N + 2 * H) // 8

    def interval(src):
        st1[...] = src[...]

        @pl.loop(0, SPAN // 2)
        def _(_):
            phi([(st1, into(st0))], cf, q0, 0, blocks, blocks)
            phi([(st0, into(st1))], cf, q0, 0, blocks, blocks)

    interval(gb)
    cc[...] = st1[:, mid, :]
    begin(further, [(cc, ca.at[:, mid], r_ca.at[1], t + 1, s)])
    for ds in (-1, 1):
        src, dst = edge(N, ds)
        begin(further & has[ds], [(cc.at[:, src], ca.at[:, dst], r_ca.at[ds + 1], t + 1, s + ds)])

    @pl.when(opening)
    def _():
        for c in opened:
            c.wait()

    arrive(jnp.logical_not(opening), [(ga.at[:, mid], r_ga.at[1])])
    for ds in (-1, 1):
        arrive(has[-ds], [(ga.at[:, edge(N, ds)[1]], r_ga.at[ds + 1])])
    interval(ga)
    cb[:, mid, :] = st1[:, mid, :]
    for ds in (-1, 1):
        src, dst = edge(N, ds)
        begin(has[ds], [(cb.at[:, shift(src, H)], cb.at[:, dst], r_cb.at[(ds + 1) // 2], t, s + ds)])

    arrive(jnp.logical_not(opening), [(ca.at[:, mid], r_ca.at[1])])
    for ds in (-1, 1):
        arrive(has[-ds], [
            (ca.at[:, edge(N, ds)[1]], r_ca.at[ds + 1]),
            (c1.at[:, edge(N1, ds)[1]], r_c1.at[(ds + 1) // 2]),
        ])
    quads(c1, q1)
    blocks1 = (N1 + 2 * H) // 8
    for k, x in enumerate(coarsen([ca[0], ca[1]], True, cmat, scr)):
        wa[k] = x

    @pl.when(first)
    def _():
        vs[:, inner, :] = wa[:, inner, :]

    begin(first, [(wa.at[:, inner], vs.at[:, inner], r_vs.at[1], base + r, s) for r in range(1, GROUP)])
    for ds in (-1, 1):
        src, dst = edge(N1, ds)
        begin(first & has[ds], [
            (wa.at[:, shift(src, H)], vs.at[:, dst], r_vs.at[ds + 1], base + r, s + ds) for r in range(GROUP)
        ])

    def forcing(which, w, r):
        slot = 2 * m + which
        last = jnp.where(m == GROUP - 1, 1.0, 0.0) if which else None

        def emit(sp, rows, cols, value):
            own = shift(rows, -H)
            g = r[sp][own, cols] - value
            if which:
                g = g - last * wc[sp, own, cols]
            gs[slot, sp, rows, cols] = g

        phi([(w, emit)], c1, q1, 1, blocks1 - 1, blocks1)
        begin(None, [
            (gs.at[slot, :, inner], gs.at[slot, :, inner], r_gs.at[slot, 1], base + to, s)
            for to in (across, partner)
        ])
        for ds in (-1, 1):
            src, dst = edge(N1, ds)
            begin(has[ds], [
                (gs.at[slot, :, shift(src, H)], gs.at[slot, :, dst], r_gs.at[slot, ds + 1], base + to, s + ds)
                for to in (across, partner, m)
            ])

    interval(ca)
    forcing(0, wa, coarsen([st1[0, mid, :], st1[1, mid, :]], False, cmat, scr))
    for k, x in enumerate(coarsen([cc[0], cc[1]], False, cmat, scr)):
        wc[k] = x
    for ds in (-1, 1):
        arrive(has[-ds], [(cb.at[:, edge(N, ds)[1]], r_cb.at[(ds + 1) // 2])])
    for k, x in enumerate(coarsen([cb[0], cb[1]], True, cmat, scr)):
        wb[k] = x
    interval(cb)
    forcing(1, wb, coarsen([st1[0, mid, :], st1[1, mid, :]], False, cmat, scr))

    for which in range(2):
        slot = 2 * across + which
        arrive(None, [(gs.at[slot, :, inner], r_gs.at[slot, 1])])
        for ds in (-1, 1):
            arrive(has[-ds], [(gs.at[slot, :, edge(N1, ds)[1]], r_gs.at[slot, ds + 1])])
        begin(None, [(gs.at[slot], gs.at[slot], r_fw.at[slot], base + partner, s)])

    arrive(jnp.logical_not(first), [(vs.at[:, inner], r_vs.at[1])])
    for ds in (-1, 1):
        arrive(has[-ds], [(vs.at[:, edge(N1, ds)[1]], r_vs.at[ds + 1])])
    vv[0] = vs[...]
    for sp, x in enumerate(coarsen([vs[0], vs[1]], True, cmat, scr)):
        zz[sp] = x
    top = (N2 + 2 * H) // 8

    def emit_old(sp, rows, cols, value):
        eo[sp, rows, cols] = -value

    def emit_new(sp, rows, cols, value):
        eo[sp, rows, cols] = eo[sp, rows, cols] + value

    phi([(zz, emit_old)], c2, q2, 1, top - 1, top)

    for which in range(2):
        slot = 2 * partner + which
        arrive(None, [(gs.at[slot, :, inner], r_gs.at[slot, 1])])
        for ds in (-1, 1):
            arrive(has[-ds], [
                (gs.at[slot, :, edge(N1, ds)[1]], r_gs.at[slot, ds + 1]),
                (gs.at[2 * m + which, :, edge(N1, ds)[1]], r_gs.at[2 * m + which, ds + 1]),
            ])
    other = lax.rem(partner + 2, GROUP)
    for which in range(2):
        slot = 2 * other + which
        arrive(None, [(gs.at[slot], r_fw.at[slot])])

    def sweep(count):
        @pl.loop(0, count)
        def _(i):
            def emit(sp, rows, cols, value):
                vv[i + 1, sp, rows, cols] = value + gs[i, sp, rows, cols]

            phi([(vv.at[i], emit)], c1, q1, 0, blocks1, blocks1)

    sweep(SPAN)

    r = coarsen([vv[SPAN, sp, inner, :] for sp in range(2)], False, cmat, scr)
    arrive(follows, [(ei.at[:, core], r_e.at[1])])
    for ds in (-1, 1):
        arrive(follows & has[-ds], [(ei.at[:, edge(N2, ds)[1]], r_e.at[ds + 1])])
    for sp in range(2):
        zy[sp] = zz[sp] + ei[sp]
    phi([(zy, emit_new)], c2, q2, 1, top - 1, top)
    for sp in range(2):
        eo[sp, core, :] = eo[sp, core, :] + r[sp]
    begin(leads, [(eo.at[:, core], ei.at[:, core], r_e.at[1], t + GROUP, s)])
    for ds in (-1, 1):
        src, dst = edge(N2, ds)
        begin(leads & has[ds], [
            (eo.at[:, shift(src, H)], ei.at[:, dst], r_e.at[ds + 1], t + GROUP, s + ds),
        ])

    p = refine([ei[0], ei[1]], emat, scr)
    for sp in range(2):
        vv[0, sp] = vs[sp] + p[sp]
    sweep(SPAN - 1)
    da = vv[2 * m, :, inner, :] - wa[:, inner, :]
    db = vv[2 * m + 1, :, inner, :] - wb[:, inner, :]
    half = H // 2
    for sp in range(2):
        ps[0, sp] = jnp.concatenate([da[sp, 0:half], db[sp, 0:half]], 0)
        ps[1, sp] = jnp.concatenate([da[sp, N1 - half :], db[sp, N1 - half :]], 0)
    for ds in (-1, 1):
        k = (ds + 1) // 2
        begin(has[ds], [(ps.at[k], pr.at[k], r_d.at[k], t, s + ds)])

    def done(i):
        return pltpu.make_async_copy(outbuf.at[i], out.at[i], s_out.at[i])

    p = refine([eo[0], eo[1]], emat, scr)
    for sp in range(2):
        vv[SPAN, sp, inner, :] = wc[sp] + p[sp][inner]
    zeros = jnp.zeros((H, c1.shape[2]), F32)
    tail = [
        jnp.concatenate([zeros, vv[2 * m + 2, sp, inner, :] - wc[sp], zeros], 0) for sp in range(2)
    ]
    p = refine(tail, emat, scr)
    for sp in range(2):
        outbuf[2 * SPAN - 1, sp] = cc[sp] + p[sp][mid]
    done(2 * SPAN - 1).start()

    for ds in (-1, 1):
        k = (ds + 1) // 2
        arrive(has[-ds], [(pr.at[k], r_d.at[k])])
    zeros = jnp.zeros((half, c1.shape[2]), F32)
    delta = []
    for which, d in enumerate((da, db)):
        rows = slice(which * half, which * half + half)
        for sp in range(2):
            delta.append(jnp.concatenate([zeros, pr[1, sp, rows, :], d[sp], pr[0, sp, rows, :], zeros], 0))
    p = refine(delta, emat, scr)
    for sp in range(2):
        st1[sp] = ca[sp] + p[sp]
        u = cb[sp] + p[2 + sp]
        gb[sp] = u
        outbuf[SPAN - 1, sp] = u[mid]
    done(SPAN - 1).start()

    def step(sources, targets, i):
        def emits(dst, at):
            def emit(sp, rows, cols, value):
                dst[sp, rows, cols] = value
                if H <= rows.start < N + H:
                    outbuf[at, sp, shift(rows, -H), cols] = value

            return emit

        at = (i, SPAN + i)
        phi([(sources[j], emits(targets[j], at[j])) for j in range(2)], cf, q0, 0, blocks, blocks)
        for j in range(2):
            done(at[j]).start()

    @pl.loop(0, 3)
    def _(k):
        step((st1, gb), (st0, ga), 2 * k)
        step((st0, ga), (st1, gb), 2 * k + 1)

    step((st1, gb), (st0, ga), SPAN - 2)
    for i in range(2 * SPAN):
        done(i).wait()
    for cond, made in sends:
        def settle():
            for c in made:
                c.wait_send()

        if cond is None:
            settle()
        else:
            pl.when(cond)(settle)


def local(T, S, initial, guess, kappa, feed, kill, react):
    _, N, C = initial.shape
    W, W1, W2 = N + 2 * H, N // 2 + 2 * H, N // 4 + 2 * H
    C1, C2 = C // 2, C // 4
    V = lambda *shape: pltpu.VMEM(shape, F32)
    D = lambda *shape: pltpu.SemaphoreType.DMA(shape)
    scratch = [
        V(5, W, C), V(2, W, C), V(5, W1, C1), V(2, W1, C1), V(5, W2, C2), V(2, W2, C2),
        V(2, W, C), V(2, W, C), V(2, W, C), V(2, W, C), V(2, N, C),
        V(2, W, C), V(2, W, C), V(2 * SPAN, 2, N, C),
        V(2, W1, C1), V(2, W1, C1), V(2, N // 2, C1), V(SPAN, 2, W1, C1), V(2, W1, C1),
        V(SPAN + 1, 2, W1, C1), V(2, 2, H, C1), V(2, 2, H, C1), V(2, W2, C2), V(2, W2, C2),
        V(2, W2, C2), V(2, W2, C2), pltpu.VMEM((C, C1), BF16), pltpu.VMEM((C1, C), BF16), V(C1 // L, 8 * W1, L),
        D(7), D(2, 4), D(2), D(3), D(2), D(3), D(2), D(3), D(SPAN, 3), D(SPAN), D(3), D(2),
        D(2 * SPAN), D(96),
    ]

    def body(*refs):
        kernel(T, S, *refs)

    return pl.pallas_call(
        body,
        out_shape=jax.ShapeDtypeStruct(guess.shape, F32),
        in_specs=[pl.BlockSpec(memory_space=pltpu.HBM)] * 6,
        out_specs=pl.BlockSpec(memory_space=pl.ANY),
        scratch_shapes=scratch,
        compiler_params=pltpu.CompilerParams(
            collective_id=0, has_side_effects=True, vmem_limit_bytes=48 * 1024 * 1024
        ),
    )(*[pltpu.with_memory_space_constraint(x, pltpu.HBM) for x in (initial, guess, kappa, feed, kill, react)])


def solution(mesh):
    T, S = mesh.shape["tm"], mesh.shape["space"]
    in_specs = (
        P(None, "space", None),
        P("tm", None, "space", None),
        P(None, "space", None),
        P("space", None),
        P("space", None),
        P("space", None),
    )
    out_specs = P("tm", None, "space", None)

    def run(*args):
        return local(T, S, *args)

    return jax.shard_map(run, mesh=mesh, in_specs=in_specs, out_specs=out_specs, check_vma=False)
```

```python
import jax
import jax.numpy as jnp
from jax import lax
from jax.experimental import pallas as pl
from jax.experimental.pallas import tpu as pltpu
from jax.sharding import PartitionSpec as P

SPAN = 8
H = 8
GROUP = SPAN // 2
MESH = pl.DeviceIdType.MESH
F32 = jnp.float32
BF16 = jnp.bfloat16
L = 128


def phi(jobs, coef, quad, first, last):
    tiles = jobs[0][0].shape[1]
    lane = lax.broadcasted_iota(jnp.int32, (8, L), 1)
    low, high = lane == 0, lane == L - 1
    cache = {}

    def load(job, b, sp, c):
        key = (job, b, sp, c)
        if key not in cache:
            x = jobs[job][0][sp, c, H + b * 8 : H + b * 8 + 8, :]
            cache[key] = (x, pltpu.roll(x, 1, 1), pltpu.roll(x, L - 1, 1))
        return cache[key]

    for blk in range(first, last):
        rows = slice(blk * 8, blk * 8 + 8)
        for c in range(tiles):
            cols = slice(c * L, c * L + L)
            k = [coef[i, rows, cols] for i in (0, 1, 2, 4)]
            q = [quad[i, rows, cols] for i in (0, 1)]
            for job, (_, emit) in enumerate(jobs):
                x, around = [], []
                for sp in range(2):
                    v, left, right = load(job, blk, sp, c)
                    at = H + blk * 8
                    above = jobs[job][0][sp, c, at - 1 : at + 7, :]
                    below = jobs[job][0][sp, c, at + 1 : at + 9, :]
                    left = jnp.where(low, load(job, blk, sp, c - 1)[1] if c > 0 else 0.0, left)
                    right = jnp.where(high, load(job, blk, sp, c + 1)[2] if c < tiles - 1 else 0.0, right)
                    x.append(v)
                    around.append((above + below) + (left + right))
                r = k[3] * x[0] * (x[1] * x[1])
                emit(0, rows, cols, q[0] * x[0] + k[0] * around[0] + (k[2] - r))
                emit(1, rows, cols, q[1] * x[1] + k[1] * around[1] + r)


def put(dst, sp, rows, cols, value):
    dst[sp, cols.start // L, rows.start + H : rows.stop + H, :] = value


def into(dst):
    return lambda sp, rows, cols, value: put(dst, sp, rows, cols, value)


def tiled(dst, src):
    for sp in range(2):
        x = src[sp]
        for c in range(dst.shape[1]):
            dst[sp, c, H : H + x.shape[0], :] = x[:, c * L : c * L + L]


def flat(src, rows):
    rows = slice(rows.start + H, rows.stop + H)
    tiles = src.shape[1]
    return [
        jnp.concatenate([src[sp, c, rows, :] for c in range(tiles)], 1) if tiles > 1 else src[sp, 0, rows, :]
        for sp in range(2)
    ]


def times(x, matrix):
    n = x.shape[0]
    a = x.astype(BF16)
    r = x - a.astype(F32)
    b = r.astype(BF16)
    c = (r - b.astype(F32)).astype(BF16)
    y = jnp.dot(jnp.concatenate([a, b, c], 0), matrix, preferred_element_type=F32)
    return y[:n] + y[n : 2 * n] + y[2 * n :]


def coarsen(xs, wide, cmat, scr):
    rows, cols = xs[0].shape
    pad = H if wide else 0
    span = rows + 2 * pad
    y = times(jnp.concatenate(xs, 0), cmat[0:cols, 0 : cols // 2])
    tiles = cols // 2 // L
    for k in range(len(xs)):
        for c in range(tiles):
            at = k * span + pad
            scr[c, at : at + rows, :] = y[k * rows : (k + 1) * rows, c * L : c * L + L]
            if pad:
                scr[c, at - pad : at, :] = jnp.zeros((pad, L), F32)
                scr[c, at + rows : at + rows + pad, :] = jnp.zeros((pad, L), F32)
    out = []
    for k in range(len(xs)):
        parts = [
            scr[c, pl.ds(k * span, span // 2, stride=2), :] + scr[c, pl.ds(k * span + 1, span // 2, stride=2), :]
            for c in range(tiles)
        ]
        out.append(0.25 * (jnp.concatenate(parts, 1) if tiles > 1 else parts[0]))
    return out


def refine(xs, emat, scr):
    rows, cols = xs[0].shape
    tiles = cols // L
    span = 2 * rows
    for k, x in enumerate(xs):
        for c in range(tiles):
            for d in range(2):
                scr[c, pl.ds(k * span + d, rows, stride=2), :] = x[:, c * L : c * L + L]
    ys = []
    for k in range(len(xs)):
        parts = [scr[c, k * span + H : (k + 1) * span - H, :] for c in range(tiles)]
        ys.append(jnp.concatenate(parts, 1) if tiles > 1 else parts[0])
    z = times(jnp.concatenate(ys, 0), emat[0:cols, 0 : 2 * cols])
    n = span - 2 * H
    return [z[k * n : (k + 1) * n] for k in range(len(xs))]


def kernel(
    T, S,
    initial, guess, kappa, feed, kill, react, out,
    cf, q0, c1, q1, c2, q2, ga, gb, ca, cb, cc, st0, st1, sb0, sb1, outbuf,
    wa, wb, wc, gs, vs, vv, ps, pr, ei, eo, zz, zy, cmat, emat, scr,
    s_loc, r_cf, r_gb, r_ga, r_c1, r_ca, r_cb, r_vs, r_gs, r_fw, r_e, r_d, s_out, s_send,
):
    t = lax.axis_index("tm")
    s = lax.axis_index("space")
    m = lax.rem(t, GROUP)
    base = t - m
    N = cf.shape[1] - 2 * H
    N1 = c1.shape[1] - 2 * H
    N2 = ei.shape[1] - 2 * H
    has = {-1: s > 0, 1: s < S - 1}
    opening = t == 0
    further = t < T - 1
    first = m == 0
    follows = base > 0
    leads = t + GROUP < T
    partner = m + 1 - 2 * lax.rem(m, 2)
    across = lax.rem(m + 2, GROUP)
    sends = []
    number = [0]

    def edge(n, ds):
        if ds == -1:
            return slice(0, H), slice(n + H, n + 2 * H)
        if ds == 1:
            return slice(n - H, n), slice(0, H)
        return slice(0, n), slice(H, n + H)

    def shift(sl, by):
        return slice(sl.start + by, sl.stop + by)

    def begin(cond, copies):
        made = []
        for src, dst, rsem, tt, ss in copies:
            made.append(pltpu.make_async_remote_copy(
                src_ref=src, dst_ref=dst, send_sem=s_send.at[number[0]], recv_sem=rsem,
                device_id=(tt, ss), device_id_type=MESH,
            ))
            number[0] += 1

        def go():
            for c in made:
                c.start()

        if cond is None:
            go()
        else:
            pl.when(cond)(go)
        sends.append((cond, made))

    def arrive(cond, waits):
        def go():
            for dst, rsem in waits:
                pltpu.make_async_copy(dst, dst, rsem).wait()

        if cond is None:
            go()
        else:
            pl.when(cond)(go)

    mid = slice(H, N + H)
    inner = slice(H, N1 + H)
    core = slice(H, N2 + H)
    local = [
        pltpu.make_async_copy(guess.at[SPAN - 1], gb.at[:, mid], s_loc.at[0]),
        pltpu.make_async_copy(kappa, cf.at[0:2, mid], s_loc.at[1]),
        pltpu.make_async_copy(feed, cf.at[2, mid], s_loc.at[2]),
        pltpu.make_async_copy(kill, cf.at[3, mid], s_loc.at[3]),
        pltpu.make_async_copy(react, cf.at[4, mid], s_loc.at[4]),
    ]
    for c in local:
        c.start()
    opened = [
        pltpu.make_async_copy(initial, ga.at[:, mid], s_loc.at[5]),
        pltpu.make_async_copy(initial, ca.at[:, mid], s_loc.at[6]),
    ]

    @pl.when(opening)
    def _():
        for c in opened:
            c.start()

    for ds in (-1, 1):
        @pl.when(jnp.logical_not(has[ds]))
        def _():
            for ref, n in ((cf, N), (ga, N), (gb, N), (ca, N), (cb, N), (c1, N1), (vs, N1)):
                rows = slice(0, H) if ds == -1 else slice(n + H, n + 2 * H)
                ref[:, rows, :] = jnp.zeros((ref.shape[0], H, ref.shape[2]), F32)
            rows = slice(0, H) if ds == -1 else slice(N1 + H, N1 + 2 * H)
            gs[:, :, rows, :] = jnp.zeros((SPAN, 2, H, gs.shape[3]), F32)
            pr[(1 - ds) // 2] = jnp.zeros(pr.shape[1:], F32)
            rows = slice(0, H) if ds == -1 else slice(N2 + H, N2 + 2 * H)
            ei[:, rows, :] = jnp.zeros((2, H, ei.shape[2]), F32)

    @pl.when(base == 0)
    def _():
        ei[...] = jnp.zeros(ei.shape, F32)

    barrier = pltpu.get_barrier_semaphore()
    count = jnp.int32(0)
    known = []
    for dt in (-GROUP, -1, 0, 1, GROUP):
        known.append((t + dt, (t + dt >= 0) & (t + dt < T), dt == 0))
    known.append((base + across, t >= 0, False))
    far = GROUP - 1 - m
    known.append((base + far, (m == 0) | (m == GROUP - 1), False))
    for other, there, own in known:
        for ds in (-1, 0, 1):
            if own and ds == 0:
                continue
            cond = there & has[ds] if ds else there

            @pl.when(cond)
            def _():
                pl.semaphore_signal(barrier, inc=1, device_id=(other, s + ds), device_id_type=MESH)

            count = count + cond.astype(jnp.int32)

    pl.semaphore_wait(barrier, count)

    for ds in (-1, 1):
        src, dst = edge(N, ds)
        k = (ds + 1) // 2
        begin(has[ds], [
            (guess.at[SPAN - 1, :, src], gb.at[:, dst], r_gb.at[k], t, s + ds),
            (kappa.at[:, src], cf.at[0:2, dst], r_cf.at[k, 0], t, s + ds),
            (feed.at[src], cf.at[2, dst], r_cf.at[k, 1], t, s + ds),
            (kill.at[src], cf.at[3, dst], r_cf.at[k, 2], t, s + ds),
            (react.at[src], cf.at[4, dst], r_cf.at[k, 3], t, s + ds),
        ])
    begin(further, [(guess.at[2 * SPAN - 1], ga.at[:, mid], r_ga.at[1], t + 1, s)])

    ii = lax.broadcasted_iota(jnp.int32, cmat.shape, 0) - 2 * lax.broadcasted_iota(jnp.int32, cmat.shape, 1)
    cmat[...] = jnp.where((ii == 0) | (ii == 1), 1.0, 0.0).astype(BF16)
    jj = lax.broadcasted_iota(jnp.int32, emat.shape, 1) - 2 * lax.broadcasted_iota(jnp.int32, emat.shape, 0)
    emat[...] = jnp.where((jj == 0) | (jj == 1), 1.0, 0.0).astype(BF16)
    eo[...] = jnp.zeros(eo.shape, F32)
    for ref, n in ((st0, N), (st1, N), (sb0, N), (sb1, N), (vv, N1), (zz, N2), (zy, N2)):
        for at in (0, n + 3 * H):
            ref[..., at : at + H, :] = jnp.zeros(ref.shape[:-2] + (H, L), F32)

    for c in local:
        c.wait()
    scale = (2.0, 2.0, 8.0, 8.0, 8.0)
    for k, x in enumerate(coarsen([cf[k, mid, :] for k in range(5)], False, cmat, scr)):
        c1[k, inner, :] = scale[k] * x
    for k, x in enumerate(coarsen([c1[k, inner, :] for k in range(5)], False, cmat, scr)):
        c2[k, core, :] = scale[k] * x
    q2[0, core, :] = 1.0 - c2[2, core, :] - 4.0 * c2[0, core, :]
    q2[1, core, :] = 1.0 - (c2[2, core, :] + c2[3, core, :]) - 4.0 * c2[1, core, :]

    for ds in (-1, 1):
        k = (ds + 1) // 2
        dst = edge(N, ds)[1]
        arrive(has[-ds], [
            (gb.at[:, dst], r_gb.at[k]),
            (cf.at[0:2, dst], r_cf.at[k, 0]),
            (cf.at[2, dst], r_cf.at[k, 1]),
            (cf.at[3, dst], r_cf.at[k, 2]),
            (cf.at[4, dst], r_cf.at[k, 3]),
        ])
    for ds in (-1, 1):
        src, dst = edge(N, ds)
        src1, dst1 = edge(N1, ds)
        begin(further & has[ds], [
            (guess.at[2 * SPAN - 1, :, src], ga.at[:, dst], r_ga.at[ds + 1], t + 1, s + ds),
        ])
        begin(opening & has[ds], [
            (initial.at[:, src], ga.at[:, dst], r_ga.at[ds + 1], t, s + ds),
            (initial.at[:, src], ca.at[:, dst], r_ca.at[ds + 1], t, s + ds),
        ])
        begin(has[ds], [
            (c1.at[:, shift(src1, H)], c1.at[:, dst1], r_c1.at[(ds + 1) // 2], t, s + ds),
        ])

    def quads(coef, quad):
        quad[0] = 1.0 - coef[2] - 4.0 * coef[0]
        quad[1] = 1.0 - (coef[2] + coef[3]) - 4.0 * coef[1]

    quads(cf, q0)
    blocks = (N + 2 * H) // 8

    def interval(src):
        tiled(st1, src)

        @pl.loop(0, SPAN // 2)
        def _(_):
            phi([(st1, into(st0))], cf, q0, 0, blocks)
            phi([(st0, into(st1))], cf, q0, 0, blocks)

    interval(gb)
    for sp, x in enumerate(flat(st1, mid)):
        cc[sp] = x
    begin(further, [(cc, ca.at[:, mid], r_ca.at[1], t + 1, s)])
    for ds in (-1, 1):
        src, dst = edge(N, ds)
        begin(further & has[ds], [(cc.at[:, src], ca.at[:, dst], r_ca.at[ds + 1], t + 1, s + ds)])

    @pl.when(opening)
    def _():
        for c in opened:
            c.wait()

    arrive(jnp.logical_not(opening), [(ga.at[:, mid], r_ga.at[1])])
    for ds in (-1, 1):
        arrive(has[-ds], [(ga.at[:, edge(N, ds)[1]], r_ga.at[ds + 1])])
    interval(ga)
    for sp, x in enumerate(flat(st1, mid)):
        cb[sp, mid, :] = x
    for ds in (-1, 1):
        src, dst = edge(N, ds)
        begin(has[ds], [(cb.at[:, shift(src, H)], cb.at[:, dst], r_cb.at[(ds + 1) // 2], t, s + ds)])

    arrive(jnp.logical_not(opening), [(ca.at[:, mid], r_ca.at[1])])
    for ds in (-1, 1):
        arrive(has[-ds], [
            (ca.at[:, edge(N, ds)[1]], r_ca.at[ds + 1]),
            (c1.at[:, edge(N1, ds)[1]], r_c1.at[(ds + 1) // 2]),
        ])
    quads(c1, q1)
    blocks1 = (N1 + 2 * H) // 8
    for k, x in enumerate(coarsen([ca[0], ca[1]], True, cmat, scr)):
        wa[k] = x

    @pl.when(first)
    def _():
        vs[:, inner, :] = wa[:, inner, :]

    begin(first, [(wa.at[:, inner], vs.at[:, inner], r_vs.at[1], base + r, s) for r in range(1, GROUP)])
    for ds in (-1, 1):
        src, dst = edge(N1, ds)
        begin(first & has[ds], [
            (wa.at[:, shift(src, H)], vs.at[:, dst], r_vs.at[ds + 1], base + r, s + ds) for r in range(GROUP)
        ])

    def forcing(which, w, r):
        slot = 2 * m + which
        last = jnp.where(m == GROUP - 1, 1.0, 0.0) if which else None

        def emit(sp, rows, cols, value):
            own = shift(rows, -H)
            g = r[sp][own, cols] - value
            if which:
                g = g - last * wc[sp, own, cols]
            gs[slot, sp, rows, cols] = g

        tiled(vv.at[SPAN], w)
        phi([(vv.at[SPAN], emit)], c1, q1, 1, blocks1 - 1)
        begin(None, [
            (gs.at[slot, :, inner], gs.at[slot, :, inner], r_gs.at[slot, 1], base + to, s)
            for to in (across, partner)
        ])
        for ds in (-1, 1):
            src, dst = edge(N1, ds)
            begin(has[ds], [
                (gs.at[slot, :, shift(src, H)], gs.at[slot, :, dst], r_gs.at[slot, ds + 1], base + to, s + ds)
                for to in (across, partner, m)
            ])

    interval(ca)
    forcing(0, wa, coarsen(flat(st1, mid), False, cmat, scr))
    for k, x in enumerate(coarsen([cc[0], cc[1]], False, cmat, scr)):
        wc[k] = x
    for ds in (-1, 1):
        arrive(has[-ds], [(cb.at[:, edge(N, ds)[1]], r_cb.at[(ds + 1) // 2])])
    for k, x in enumerate(coarsen([cb[0], cb[1]], True, cmat, scr)):
        wb[k] = x
    interval(cb)
    forcing(1, wb, coarsen(flat(st1, mid), False, cmat, scr))

    for which in range(2):
        slot = 2 * across + which
        arrive(None, [(gs.at[slot, :, inner], r_gs.at[slot, 1])])
        for ds in (-1, 1):
            arrive(has[-ds], [(gs.at[slot, :, edge(N1, ds)[1]], r_gs.at[slot, ds + 1])])
        begin(None, [(gs.at[slot], gs.at[slot], r_fw.at[slot], base + partner, s)])

    arrive(jnp.logical_not(first), [(vs.at[:, inner], r_vs.at[1])])
    for ds in (-1, 1):
        arrive(has[-ds], [(vs.at[:, edge(N1, ds)[1]], r_vs.at[ds + 1])])
    tiled(vv.at[0], vs)
    for sp, x in enumerate(coarsen([vs[0], vs[1]], True, cmat, scr)):
        zz[sp, 0, H : H + x.shape[0], :] = x
    top = (N2 + 2 * H) // 8

    def emit_old(sp, rows, cols, value):
        eo[sp, rows, cols] = -value

    def emit_new(sp, rows, cols, value):
        eo[sp, rows, cols] = eo[sp, rows, cols] + value

    phi([(zz, emit_old)], c2, q2, 1, top - 1)

    for which in range(2):
        slot = 2 * partner + which
        arrive(None, [(gs.at[slot, :, inner], r_gs.at[slot, 1])])
        for ds in (-1, 1):
            arrive(has[-ds], [
                (gs.at[slot, :, edge(N1, ds)[1]], r_gs.at[slot, ds + 1]),
                (gs.at[2 * m + which, :, edge(N1, ds)[1]], r_gs.at[2 * m + which, ds + 1]),
            ])
    other = lax.rem(partner + 2, GROUP)
    for which in range(2):
        slot = 2 * other + which
        arrive(None, [(gs.at[slot], r_fw.at[slot])])

    def sweep(count):
        @pl.loop(0, count)
        def _(i):
            def emit(sp, rows, cols, value):
                put(vv.at[i + 1], sp, rows, cols, value + gs[i, sp, rows, cols])

            phi([(vv.at[i], emit)], c1, q1, 0, blocks1)

    sweep(SPAN)

    r = coarsen(flat(vv.at[SPAN], inner), False, cmat, scr)
    arrive(follows, [(ei.at[:, core], r_e.at[1])])
    for ds in (-1, 1):
        arrive(follows & has[-ds], [(ei.at[:, edge(N2, ds)[1]], r_e.at[ds + 1])])
    for sp in range(2):
        zy[sp, 0, H : H + ei.shape[1], :] = zz[sp, 0, H : H + ei.shape[1], :] + ei[sp]
    phi([(zy, emit_new)], c2, q2, 1, top - 1)
    for sp in range(2):
        eo[sp, core, :] = eo[sp, core, :] + r[sp]
    begin(leads, [(eo.at[:, core], ei.at[:, core], r_e.at[1], t + GROUP, s)])
    for ds in (-1, 1):
        src, dst = edge(N2, ds)
        begin(leads & has[ds], [
            (eo.at[:, shift(src, H)], ei.at[:, dst], r_e.at[ds + 1], t + GROUP, s + ds),
        ])

    p = refine([ei[0], ei[1]], emat, scr)
    for sp in range(2):
        p[sp] = vs[sp] + p[sp]
    tiled(vv.at[0], p)
    sweep(SPAN - 1)
    da = [x - wa[sp, inner, :] for sp, x in enumerate(flat(vv.at[2 * m], inner))]
    db = [x - wb[sp, inner, :] for sp, x in enumerate(flat(vv.at[2 * m + 1], inner))]
    half = H // 2
    for sp in range(2):
        ps[0, sp] = jnp.concatenate([da[sp][0:half], db[sp][0:half]], 0)
        ps[1, sp] = jnp.concatenate([da[sp][N1 - half :], db[sp][N1 - half :]], 0)
    for ds in (-1, 1):
        k = (ds + 1) // 2
        begin(has[ds], [(ps.at[k], pr.at[k], r_d.at[k], t, s + ds)])

    def done(i):
        return pltpu.make_async_copy(outbuf.at[i], out.at[i], s_out.at[i])

    p = refine([eo[0], eo[1]], emat, scr)
    for sp in range(2):
        x = wc[sp] + p[sp][inner]
        for c in range(vv.shape[2]):
            vv[SPAN, sp, c, 2 * H : 2 * H + N1, :] = x[:, c * L : c * L + L]
    zeros = jnp.zeros((H, c1.shape[2]), F32)
    last = flat(vv.at[2 * m + 2], inner)
    tail = [jnp.concatenate([zeros, last[sp] - wc[sp], zeros], 0) for sp in range(2)]
    p = refine(tail, emat, scr)
    for sp in range(2):
        outbuf[2 * SPAN - 1, sp] = cc[sp] + p[sp][mid]
    done(2 * SPAN - 1).start()

    for ds in (-1, 1):
        k = (ds + 1) // 2
        arrive(has[-ds], [(pr.at[k], r_d.at[k])])
    zeros = jnp.zeros((half, c1.shape[2]), F32)
    delta = []
    for which, d in enumerate((da, db)):
        rows = slice(which * half, which * half + half)
        for sp in range(2):
            delta.append(jnp.concatenate([zeros, pr[1, sp, rows, :], d[sp], pr[0, sp, rows, :], zeros], 0))
    p = refine(delta, emat, scr)
    for sp in range(2):
        u = cb[sp] + p[2 + sp]
        for c in range(st1.shape[1]):
            st1[sp, c, H : H + u.shape[0], :] = ca[sp, :, c * L : c * L + L] + p[sp][:, c * L : c * L + L]
            sb1[sp, c, H : H + u.shape[0], :] = u[:, c * L : c * L + L]
        outbuf[SPAN - 1, sp] = u[mid]
    done(SPAN - 1).start()

    def step(sources, targets, i):
        def emits(dst, at):
            def emit(sp, rows, cols, value):
                put(dst, sp, rows, cols, value)
                if H <= rows.start < N + H:
                    outbuf[at, sp, shift(rows, -H), cols] = value

            return emit

        at = (i, SPAN + i)
        phi([(sources[j], emits(targets[j], at[j])) for j in range(2)], cf, q0, 0, blocks)
        for j in range(2):
            done(at[j]).start()

    @pl.loop(0, 3)
    def _(k):
        step((st1, sb1), (st0, sb0), 2 * k)
        step((st0, sb0), (st1, sb1), 2 * k + 1)

    step((st1, sb1), (st0, sb0), SPAN - 2)
    for i in range(2 * SPAN):
        done(i).wait()
    for cond, made in sends:
        def settle():
            for c in made:
                c.wait_send()

        if cond is None:
            settle()
        else:
            pl.when(cond)(settle)


def local(T, S, initial, guess, kappa, feed, kill, react):
    _, N, C = initial.shape
    W, W1, W2 = N + 2 * H, N // 2 + 2 * H, N // 4 + 2 * H
    C1, C2 = C // 2, C // 4
    V = lambda *shape: pltpu.VMEM(shape, F32)
    D = lambda *shape: pltpu.SemaphoreType.DMA(shape)
    scratch = [
        V(5, W, C), V(2, W, C), V(5, W1, C1), V(2, W1, C1), V(5, W2, C2), V(2, W2, C2),
        V(2, W, C), V(2, W, C), V(2, W, C), V(2, W, C), V(2, N, C),
        *[V(2, C // L, W + 2 * H, L) for _ in range(4)], V(2 * SPAN, 2, N, C),
        V(2, W1, C1), V(2, W1, C1), V(2, N // 2, C1), V(SPAN, 2, W1, C1), V(2, W1, C1),
        V(SPAN + 1, 2, C1 // L, W1 + 2 * H, L), V(2, 2, H, C1), V(2, 2, H, C1), V(2, W2, C2), V(2, W2, C2),
        V(2, C2 // L, W2 + 2 * H, L), V(2, C2 // L, W2 + 2 * H, L), pltpu.VMEM((C, C1), BF16), pltpu.VMEM((C1, C), BF16), V(C1 // L, 8 * W1, L),
        D(7), D(2, 4), D(2), D(3), D(2), D(3), D(2), D(3), D(SPAN, 3), D(SPAN), D(3), D(2),
        D(2 * SPAN), D(96),
    ]

    def body(*refs):
        kernel(T, S, *refs)

    return pl.pallas_call(
        body,
        out_shape=jax.ShapeDtypeStruct(guess.shape, F32),
        in_specs=[pl.BlockSpec(memory_space=pltpu.HBM)] * 6,
        out_specs=pl.BlockSpec(memory_space=pl.ANY),
        scratch_shapes=scratch,
        compiler_params=pltpu.CompilerParams(
            collective_id=0, has_side_effects=True, vmem_limit_bytes=48 * 1024 * 1024
        ),
    )(*[pltpu.with_memory_space_constraint(x, pltpu.HBM) for x in (initial, guess, kappa, feed, kill, react)])


def solution(mesh):
    T, S = mesh.shape["tm"], mesh.shape["space"]
    in_specs = (
        P(None, "space", None),
        P("tm", None, "space", None),
        P(None, "space", None),
        P("space", None),
        P("space", None),
        P("space", None),
    )
    out_specs = P("tm", None, "space", None)

    def run(*args):
        return local(T, S, *args)

    return jax.shard_map(run, mesh=mesh, in_specs=in_specs, out_specs=out_specs, check_vma=False)
```

```python
import jax
import jax.numpy as jnp
from jax import lax
from jax.experimental import pallas as pl
from jax.experimental.pallas import tpu as pltpu
from jax.sharding import PartitionSpec as P

SPAN = 8
H = 8
GROUP = SPAN // 2
MESH = pl.DeviceIdType.MESH
F32 = jnp.float32
BF16 = jnp.bfloat16
L = 128


def phi(jobs, coef, quad, first, last):
    tiles = jobs[0][0].shape[1]
    lane = lax.broadcasted_iota(jnp.int32, (8, L), 1)
    low, high = lane == 0, lane == L - 1
    cache = {}

    def load(job, b, sp, c):
        key = (job, b, sp, c)
        if key not in cache:
            x = jobs[job][0][sp, c, H + b * 8 : H + b * 8 + 8, :]
            cache[key] = (x, pltpu.roll(x, 1, 1), pltpu.roll(x, L - 1, 1))
        return cache[key]

    for blk in range(first, last):
        rows = slice(blk * 8, blk * 8 + 8)
        for c in range(tiles):
            cols = slice(c * L, c * L + L)
            k = [coef[i, rows, cols] for i in (0, 1, 2, 4)]
            q = [quad[i, rows, cols] for i in (0, 1)]
            for job, (_, emit) in enumerate(jobs):
                x, around = [], []
                for sp in range(2):
                    v, left, right = load(job, blk, sp, c)
                    at = H + blk * 8
                    above = jobs[job][0][sp, c, at - 1 : at + 7, :]
                    below = jobs[job][0][sp, c, at + 1 : at + 9, :]
                    left = jnp.where(low, load(job, blk, sp, c - 1)[1] if c > 0 else 0.0, left)
                    right = jnp.where(high, load(job, blk, sp, c + 1)[2] if c < tiles - 1 else 0.0, right)
                    x.append(v)
                    around.append((above + below) + (left + right))
                r = k[3] * x[0] * (x[1] * x[1])
                emit(0, rows, cols, q[0] * x[0] + k[0] * around[0] + (k[2] - r))
                emit(1, rows, cols, q[1] * x[1] + k[1] * around[1] + r)


def put(dst, sp, rows, cols, value):
    dst[sp, cols.start // L, rows.start + H : rows.stop + H, :] = value


def into(dst):
    return lambda sp, rows, cols, value: put(dst, sp, rows, cols, value)


def tiled(dst, src):
    for sp in range(2):
        x = src[sp]
        for c in range(dst.shape[1]):
            dst[sp, c, H : H + x.shape[0], :] = x[:, c * L : c * L + L]


def flat(src, rows):
    rows = slice(rows.start + H, rows.stop + H)
    tiles = src.shape[1]
    return [
        jnp.concatenate([src[sp, c, rows, :] for c in range(tiles)], 1) if tiles > 1 else src[sp, 0, rows, :]
        for sp in range(2)
    ]


def times(x, matrix):
    n = x.shape[0]
    a = x.astype(BF16)
    r = x - a.astype(F32)
    b = r.astype(BF16)
    c = (r - b.astype(F32)).astype(BF16)
    y = jnp.dot(jnp.concatenate([a, b, c], 0), matrix, preferred_element_type=F32)
    return y[:n] + y[n : 2 * n] + y[2 * n :]


def coarsen(xs, wide, cmat, scr):
    rows, cols = xs[0].shape
    pad = H if wide else 0
    span = rows + 2 * pad
    y = times(jnp.concatenate(xs, 0), cmat[0:cols, 0 : cols // 2])
    tiles = cols // 2 // L
    for k in range(len(xs)):
        for c in range(tiles):
            at = k * span + pad
            scr[c, at : at + rows, :] = y[k * rows : (k + 1) * rows, c * L : c * L + L]
            if pad:
                scr[c, at - pad : at, :] = jnp.zeros((pad, L), F32)
                scr[c, at + rows : at + rows + pad, :] = jnp.zeros((pad, L), F32)
    out = []
    for k in range(len(xs)):
        parts = [
            scr[c, pl.ds(k * span, span // 2, stride=2), :] + scr[c, pl.ds(k * span + 1, span // 2, stride=2), :]
            for c in range(tiles)
        ]
        out.append(0.25 * (jnp.concatenate(parts, 1) if tiles > 1 else parts[0]))
    return out


def refine(xs, emat, scr):
    rows, cols = xs[0].shape
    tiles = cols // L
    span = 2 * rows
    for k, x in enumerate(xs):
        for c in range(tiles):
            for d in range(2):
                scr[c, pl.ds(k * span + d, rows, stride=2), :] = x[:, c * L : c * L + L]
    ys = []
    for k in range(len(xs)):
        parts = [scr[c, k * span + H : (k + 1) * span - H, :] for c in range(tiles)]
        ys.append(jnp.concatenate(parts, 1) if tiles > 1 else parts[0])
    z = times(jnp.concatenate(ys, 0), emat[0:cols, 0 : 2 * cols])
    n = span - 2 * H
    return [z[k * n : (k + 1) * n] for k in range(len(xs))]


def kernel(
    T, S,
    initial, guess, kappa, feed, kill, react, out,
    cf, q0, c1, q1, c2, q2, ga, gb, ca, cb, cc, st0, st1, sb0, sb1, outbuf,
    wa, wb, wc, gs, vs, vv, ps, pr, ei, eo, zz, zy, cmat, emat, scr,
    s_loc, r_cf, r_gb, r_ga, r_c1, r_ca, r_cb, r_vs, r_gs, r_fw, r_e, r_d, s_out, s_send,
):
    t = lax.axis_index("tm")
    s = lax.axis_index("space")
    m = lax.rem(t, GROUP)
    base = t - m
    N = cf.shape[1] - 2 * H
    N1 = c1.shape[1] - 2 * H
    N2 = ei.shape[1] - 2 * H
    has = {-1: s > 0, 1: s < S - 1}
    opening = t == 0
    further = t < T - 1
    first = m == 0
    follows = base > 0
    leads = t + GROUP < T
    partner = m + 1 - 2 * lax.rem(m, 2)
    across = lax.rem(m + 2, GROUP)
    sends = []
    number = [0]

    def edge(n, ds):
        if ds == -1:
            return slice(0, H), slice(n + H, n + 2 * H)
        if ds == 1:
            return slice(n - H, n), slice(0, H)
        return slice(0, n), slice(H, n + H)

    def shift(sl, by):
        return slice(sl.start + by, sl.stop + by)

    def begin(cond, copies):
        made = []
        for src, dst, rsem, tt, ss in copies:
            made.append(pltpu.make_async_remote_copy(
                src_ref=src, dst_ref=dst, send_sem=s_send.at[number[0]], recv_sem=rsem,
                device_id=(tt, ss), device_id_type=MESH,
            ))
            number[0] += 1

        def go():
            for c in made:
                c.start()

        if cond is None:
            go()
        else:
            pl.when(cond)(go)
        sends.append((cond, made))

    def arrive(cond, waits):
        def go():
            for dst, rsem in waits:
                pltpu.make_async_copy(dst, dst, rsem).wait()

        if cond is None:
            go()
        else:
            pl.when(cond)(go)

    mid = slice(H, N + H)
    inner = slice(H, N1 + H)
    core = slice(H, N2 + H)
    local = [
        pltpu.make_async_copy(guess.at[SPAN - 1], gb.at[:, mid], s_loc.at[0]),
        pltpu.make_async_copy(kappa, cf.at[0:2, mid], s_loc.at[1]),
        pltpu.make_async_copy(feed, cf.at[2, mid], s_loc.at[2]),
        pltpu.make_async_copy(kill, cf.at[3, mid], s_loc.at[3]),
        pltpu.make_async_copy(react, cf.at[4, mid], s_loc.at[4]),
    ]
    for c in local:
        c.start()
    opened = [
        pltpu.make_async_copy(initial, ga.at[:, mid], s_loc.at[5]),
        pltpu.make_async_copy(initial, ca.at[:, mid], s_loc.at[6]),
    ]

    @pl.when(opening)
    def _():
        for c in opened:
            c.start()

    for ds in (-1, 1):
        @pl.when(jnp.logical_not(has[ds]))
        def _():
            for ref, n in ((cf, N), (ga, N), (gb, N), (ca, N), (cb, N), (c1, N1), (vs, N1)):
                rows = slice(0, H) if ds == -1 else slice(n + H, n + 2 * H)
                ref[:, rows, :] = jnp.zeros((ref.shape[0], H, ref.shape[2]), F32)
            rows = slice(0, H) if ds == -1 else slice(N1 + H, N1 + 2 * H)
            gs[:, :, rows, :] = jnp.zeros((SPAN, 2, H, gs.shape[3]), F32)
            pr[(1 - ds) // 2] = jnp.zeros(pr.shape[1:], F32)
            rows = slice(0, H) if ds == -1 else slice(N2 + H, N2 + 2 * H)
            ei[:, rows, :] = jnp.zeros((2, H, ei.shape[2]), F32)

    @pl.when(base == 0)
    def _():
        ei[...] = jnp.zeros(ei.shape, F32)

    barrier = pltpu.get_barrier_semaphore()
    count = jnp.int32(0)
    known = []
    for dt in (-GROUP, -1, 0, 1, GROUP):
        known.append((t + dt, (t + dt >= 0) & (t + dt < T), dt == 0))
    known.append((base + across, t >= 0, False))
    far = GROUP - 1 - m
    known.append((base + far, (m == 0) | (m == GROUP - 1), False))
    for other, there, own in known:
        for ds in (-1, 0, 1):
            if own and ds == 0:
                continue
            cond = there & has[ds] if ds else there

            @pl.when(cond)
            def _():
                pl.semaphore_signal(barrier, inc=1, device_id=(other, s + ds), device_id_type=MESH)

            count = count + cond.astype(jnp.int32)

    pl.semaphore_wait(barrier, count)

    for ds in (-1, 1):
        src, dst = edge(N, ds)
        k = (ds + 1) // 2
        begin(has[ds], [
            (guess.at[SPAN - 1, :, src], gb.at[:, dst], r_gb.at[k], t, s + ds),
            (kappa.at[:, src], cf.at[0:2, dst], r_cf.at[k, 0], t, s + ds),
            (feed.at[src], cf.at[2, dst], r_cf.at[k, 1], t, s + ds),
            (kill.at[src], cf.at[3, dst], r_cf.at[k, 2], t, s + ds),
            (react.at[src], cf.at[4, dst], r_cf.at[k, 3], t, s + ds),
        ])
    begin(further, [(guess.at[2 * SPAN - 1], ga.at[:, mid], r_ga.at[1], t + 1, s)])

    ii = lax.broadcasted_iota(jnp.int32, cmat.shape, 0) - 2 * lax.broadcasted_iota(jnp.int32, cmat.shape, 1)
    cmat[...] = jnp.where((ii == 0) | (ii == 1), 1.0, 0.0).astype(BF16)
    jj = lax.broadcasted_iota(jnp.int32, emat.shape, 1) - 2 * lax.broadcasted_iota(jnp.int32, emat.shape, 0)
    emat[...] = jnp.where((jj == 0) | (jj == 1), 1.0, 0.0).astype(BF16)
    eo[...] = jnp.zeros(eo.shape, F32)
    for ref, n in ((st0, N), (st1, N), (sb0, N), (sb1, N), (vv, N1), (zz, N2), (zy, N2)):
        for at in (0, n + 3 * H):
            ref[..., at : at + H, :] = jnp.zeros(ref.shape[:-2] + (H, L), F32)

    for c in local:
        c.wait()
    scale = (2.0, 2.0, 8.0, 8.0, 8.0)
    for k, x in enumerate(coarsen([cf[k, mid, :] for k in range(5)], False, cmat, scr)):
        c1[k, inner, :] = scale[k] * x
    for k, x in enumerate(coarsen([c1[k, inner, :] for k in range(5)], False, cmat, scr)):
        c2[k, core, :] = scale[k] * x
    q2[0, core, :] = 1.0 - c2[2, core, :] - 4.0 * c2[0, core, :]
    q2[1, core, :] = 1.0 - (c2[2, core, :] + c2[3, core, :]) - 4.0 * c2[1, core, :]

    for ds in (-1, 1):
        k = (ds + 1) // 2
        dst = edge(N, ds)[1]
        arrive(has[-ds], [
            (gb.at[:, dst], r_gb.at[k]),
            (cf.at[0:2, dst], r_cf.at[k, 0]),
            (cf.at[2, dst], r_cf.at[k, 1]),
            (cf.at[3, dst], r_cf.at[k, 2]),
            (cf.at[4, dst], r_cf.at[k, 3]),
        ])
    for ds in (-1, 1):
        src, dst = edge(N, ds)
        begin(further & has[ds], [
            (guess.at[2 * SPAN - 1, :, src], ga.at[:, dst], r_ga.at[ds + 1], t + 1, s + ds),
        ])
        begin(opening & has[ds], [
            (initial.at[:, src], ga.at[:, dst], r_ga.at[ds + 1], t, s + ds),
            (initial.at[:, src], ca.at[:, dst], r_ca.at[ds + 1], t, s + ds),
        ])

    def quads(coef, quad):
        quad[0] = 1.0 - coef[2] - 4.0 * coef[0]
        quad[1] = 1.0 - (coef[2] + coef[3]) - 4.0 * coef[1]

    quads(cf, q0)
    blocks = (N + 2 * H) // 8

    def interval(src):
        tiled(st1, src)

        @pl.loop(0, SPAN // 2)
        def _(_):
            phi([(st1, into(st0))], cf, q0, 0, blocks)
            phi([(st0, into(st1))], cf, q0, 0, blocks)

    interval(gb)
    for sp, x in enumerate(flat(st1, mid)):
        cc[sp] = x
    begin(further, [(cc, ca.at[:, mid], r_ca.at[1], t + 1, s)])
    for ds in (-1, 1):
        src, dst = edge(N, ds)
        begin(further & has[ds], [(cc.at[:, src], ca.at[:, dst], r_ca.at[ds + 1], t + 1, s + ds)])

    @pl.when(opening)
    def _():
        for c in opened:
            c.wait()

    arrive(jnp.logical_not(opening), [(ga.at[:, mid], r_ga.at[1])])
    for ds in (-1, 1):
        arrive(has[-ds], [(ga.at[:, edge(N, ds)[1]], r_ga.at[ds + 1])])
    interval(ga)
    for sp, x in enumerate(flat(st1, mid)):
        cb[sp, mid, :] = x
    for ds in (-1, 1):
        src, dst = edge(N, ds)
        begin(has[ds], [(cb.at[:, shift(src, H)], cb.at[:, dst], r_cb.at[(ds + 1) // 2], t, s + ds)])

    arrive(jnp.logical_not(opening), [(ca.at[:, mid], r_ca.at[1])])
    for ds in (-1, 1):
        arrive(has[-ds], [(ca.at[:, edge(N, ds)[1]], r_ca.at[ds + 1])])
    quads(c1.at[:, inner], q1.at[:, inner])
    blocks1 = (N1 + 2 * H) // 8
    for k, x in enumerate(coarsen([ca[0], ca[1]], True, cmat, scr)):
        wa[k] = x

    @pl.when(first)
    def _():
        vs[:, inner, :] = wa[:, inner, :]

    for ds in (-1, 1):
        src, dst = edge(N1, ds)
        begin(first & has[ds], [(wa.at[:, shift(src, H)], vs.at[:, dst], r_vs.at[ds + 1], t, s + ds)])

    def forcing(which, w, r):
        slot = 2 * m + which
        last = jnp.where(m == GROUP - 1, 1.0, 0.0) if which else None

        def emit(sp, rows, cols, value):
            own = shift(rows, -H)
            g = r[sp][own, cols] - value
            if which:
                g = g - last * wc[sp, own, cols]
            gs[slot, sp, rows, cols] = g

        tiled(vv.at[SPAN], w)
        phi([(vv.at[SPAN], emit)], c1, q1, 1, blocks1 - 1)
        for ds in (-1, 1):
            src, dst = edge(N1, ds)
            begin(has[ds], [(gs.at[slot, :, shift(src, H)], gs.at[slot, :, dst], r_gs.at[slot, ds + 1], t, s + ds)])

    def spread(which):
        slot = 2 * m + which
        for ds in (-1, 1):
            arrive(has[-ds], [(gs.at[slot, :, edge(N1, ds)[1]], r_gs.at[slot, ds + 1])])
        begin(None, [(gs.at[slot], gs.at[slot], r_gs.at[slot, 1], base + to, s) for to in (across, partner)])

    interval(ca)
    forcing(0, wa, coarsen(flat(st1, mid), False, cmat, scr))
    for k, x in enumerate(coarsen([cc[0], cc[1]], False, cmat, scr)):
        wc[k] = x
    for ds in (-1, 1):
        arrive(has[-ds], [(cb.at[:, edge(N, ds)[1]], r_cb.at[(ds + 1) // 2])])
    for k, x in enumerate(coarsen([cb[0], cb[1]], True, cmat, scr)):
        wb[k] = x
    spread(0)
    for ds in (-1, 1):
        arrive(first & has[-ds], [(vs.at[:, edge(N1, ds)[1]], r_vs.at[ds + 1])])
    begin(first, [(vs, vs, r_vs.at[1], base + r, s) for r in range(1, GROUP)])
    for ds in (-1, 1):
        src, dst = edge(N1, ds)
        begin(has[ds], [
            (c1.at[:, shift(src, H)], c1.at[:, dst], r_c1.at[(ds + 1) // 2], t, s + ds),
        ])
    interval(cb)
    forcing(1, wb, coarsen(flat(st1, mid), False, cmat, scr))

    spread(1)

    for which in range(2):
        slot = 2 * across + which
        arrive(None, [(gs.at[slot], r_gs.at[slot, 1])])
        begin(None, [(gs.at[slot], gs.at[slot], r_fw.at[slot], base + partner, s)])

    arrive(jnp.logical_not(first), [(vs, r_vs.at[1])])
    tiled(vv.at[0], vs)
    for sp, x in enumerate(coarsen([vs[0], vs[1]], True, cmat, scr)):
        zz[sp, 0, H : H + x.shape[0], :] = x
    top = (N2 + 2 * H) // 8

    def emit_old(sp, rows, cols, value):
        eo[sp, rows, cols] = -value

    def emit_new(sp, rows, cols, value):
        eo[sp, rows, cols] = eo[sp, rows, cols] + value

    phi([(zz, emit_old)], c2, q2, 1, top - 1)

    for ds in (-1, 1):
        arrive(has[-ds], [(c1.at[:, edge(N1, ds)[1]], r_c1.at[(ds + 1) // 2])])
    quads(c1, q1)
    for which in range(2):
        slot = 2 * partner + which
        arrive(None, [(gs.at[slot], r_gs.at[slot, 1])])
    other = lax.rem(partner + 2, GROUP)
    for which in range(2):
        slot = 2 * other + which
        arrive(None, [(gs.at[slot], r_fw.at[slot])])

    def sweep(count):
        @pl.loop(0, count)
        def _(i):
            def emit(sp, rows, cols, value):
                put(vv.at[i + 1], sp, rows, cols, value + gs[i, sp, rows, cols])

            phi([(vv.at[i], emit)], c1, q1, 0, blocks1)

    sweep(SPAN)

    r = coarsen(flat(vv.at[SPAN], inner), False, cmat, scr)
    arrive(follows, [(ei.at[:, core], r_e.at[1])])
    for ds in (-1, 1):
        arrive(follows & has[-ds], [(ei.at[:, edge(N2, ds)[1]], r_e.at[ds + 1])])
    for sp in range(2):
        zy[sp, 0, H : H + ei.shape[1], :] = zz[sp, 0, H : H + ei.shape[1], :] + ei[sp]
    phi([(zy, emit_new)], c2, q2, 1, top - 1)
    for sp in range(2):
        eo[sp, core, :] = eo[sp, core, :] + r[sp]
    begin(leads, [(eo.at[:, core], ei.at[:, core], r_e.at[1], t + GROUP, s)])
    for ds in (-1, 1):
        src, dst = edge(N2, ds)
        begin(leads & has[ds], [
            (eo.at[:, shift(src, H)], ei.at[:, dst], r_e.at[ds + 1], t + GROUP, s + ds),
        ])

    p = refine([ei[0], ei[1]], emat, scr)
    for sp in range(2):
        p[sp] = vs[sp] + p[sp]
    tiled(vv.at[0], p)
    sweep(SPAN - 1)
    da = [x - wa[sp, inner, :] for sp, x in enumerate(flat(vv.at[2 * m], inner))]
    db = [x - wb[sp, inner, :] for sp, x in enumerate(flat(vv.at[2 * m + 1], inner))]
    half = H // 2
    for sp in range(2):
        ps[0, sp] = jnp.concatenate([da[sp][0:half], db[sp][0:half]], 0)
        ps[1, sp] = jnp.concatenate([da[sp][N1 - half :], db[sp][N1 - half :]], 0)
    for ds in (-1, 1):
        k = (ds + 1) // 2
        begin(has[ds], [(ps.at[k], pr.at[k], r_d.at[k], t, s + ds)])

    def done(i):
        return pltpu.make_async_copy(outbuf.at[i], out.at[i], s_out.at[i])

    p = refine([eo[0], eo[1]], emat, scr)
    for sp in range(2):
        x = wc[sp] + p[sp][inner]
        for c in range(vv.shape[2]):
            vv[SPAN, sp, c, 2 * H : 2 * H + N1, :] = x[:, c * L : c * L + L]
    zeros = jnp.zeros((H, c1.shape[2]), F32)
    last = flat(vv.at[2 * m + 2], inner)
    tail = [jnp.concatenate([zeros, last[sp] - wc[sp], zeros], 0) for sp in range(2)]
    p = refine(tail, emat, scr)
    for sp in range(2):
        outbuf[2 * SPAN - 1, sp] = cc[sp] + p[sp][mid]
    done(2 * SPAN - 1).start()

    for ds in (-1, 1):
        k = (ds + 1) // 2
        arrive(has[-ds], [(pr.at[k], r_d.at[k])])
    zeros = jnp.zeros((half, c1.shape[2]), F32)
    delta = []
    for which, d in enumerate((da, db)):
        rows = slice(which * half, which * half + half)
        for sp in range(2):
            delta.append(jnp.concatenate([zeros, pr[1, sp, rows, :], d[sp], pr[0, sp, rows, :], zeros], 0))
    p = refine(delta, emat, scr)
    for sp in range(2):
        u = cb[sp] + p[2 + sp]
        for c in range(st1.shape[1]):
            st1[sp, c, H : H + u.shape[0], :] = ca[sp, :, c * L : c * L + L] + p[sp][:, c * L : c * L + L]
            sb1[sp, c, H : H + u.shape[0], :] = u[:, c * L : c * L + L]
        outbuf[SPAN - 1, sp] = u[mid]
    done(SPAN - 1).start()

    def step(sources, targets, i):
        def emits(dst, at):
            def emit(sp, rows, cols, value):
                put(dst, sp, rows, cols, value)
                if H <= rows.start < N + H:
                    outbuf[at, sp, shift(rows, -H), cols] = value

            return emit

        at = (i, SPAN + i)
        phi([(sources[j], emits(targets[j], at[j])) for j in range(2)], cf, q0, 0, blocks)
        for j in range(2):
            done(at[j]).start()

    @pl.loop(0, 3)
    def _(k):
        step((st1, sb1), (st0, sb0), 2 * k)
        step((st0, sb0), (st1, sb1), 2 * k + 1)

    step((st1, sb1), (st0, sb0), SPAN - 2)
    for i in range(2 * SPAN):
        done(i).wait()
    for cond, made in sends:
        def settle():
            for c in made:
                c.wait_send()

        if cond is None:
            settle()
        else:
            pl.when(cond)(settle)


def local(T, S, initial, guess, kappa, feed, kill, react):
    _, N, C = initial.shape
    W, W1, W2 = N + 2 * H, N // 2 + 2 * H, N // 4 + 2 * H
    C1, C2 = C // 2, C // 4
    V = lambda *shape: pltpu.VMEM(shape, F32)
    D = lambda *shape: pltpu.SemaphoreType.DMA(shape)
    scratch = [
        V(5, W, C), V(2, W, C), V(5, W1, C1), V(2, W1, C1), V(5, W2, C2), V(2, W2, C2),
        V(2, W, C), V(2, W, C), V(2, W, C), V(2, W, C), V(2, N, C),
        *[V(2, C // L, W + 2 * H, L) for _ in range(4)], V(2 * SPAN, 2, N, C),
        V(2, W1, C1), V(2, W1, C1), V(2, N // 2, C1), V(SPAN, 2, W1, C1), V(2, W1, C1),
        V(SPAN + 1, 2, C1 // L, W1 + 2 * H, L), V(2, 2, H, C1), V(2, 2, H, C1), V(2, W2, C2), V(2, W2, C2),
        V(2, C2 // L, W2 + 2 * H, L), V(2, C2 // L, W2 + 2 * H, L), pltpu.VMEM((C, C1), BF16), pltpu.VMEM((C1, C), BF16), V(C1 // L, 8 * W1, L),
        D(7), D(2, 4), D(2), D(3), D(2), D(3), D(2), D(3), D(SPAN, 3), D(SPAN), D(3), D(2),
        D(2 * SPAN), D(96),
    ]

    def body(*refs):
        kernel(T, S, *refs)

    return pl.pallas_call(
        body,
        out_shape=jax.ShapeDtypeStruct(guess.shape, F32),
        in_specs=[pl.BlockSpec(memory_space=pltpu.HBM)] * 6,
        out_specs=pl.BlockSpec(memory_space=pl.ANY),
        scratch_shapes=scratch,
        compiler_params=pltpu.CompilerParams(
            collective_id=0, has_side_effects=True, vmem_limit_bytes=48 * 1024 * 1024
        ),
    )(*[pltpu.with_memory_space_constraint(x, pltpu.HBM) for x in (initial, guess, kappa, feed, kill, react)])


def solution(mesh):
    T, S = mesh.shape["tm"], mesh.shape["space"]
    in_specs = (
        P(None, "space", None),
        P("tm", None, "space", None),
        P(None, "space", None),
        P("space", None),
        P("space", None),
        P("space", None),
    )
    out_specs = P("tm", None, "space", None)

    def run(*args):
        return local(T, S, *args)

    return jax.shard_map(run, mesh=mesh, in_specs=in_specs, out_specs=out_specs, check_vma=False)
```

```python
import jax
import jax.numpy as jnp
from jax import lax
from jax.experimental import pallas as pl
from jax.experimental.pallas import tpu as pltpu
from jax.sharding import PartitionSpec as P

SPAN = 8
H = 8
GROUP = SPAN // 2
MESH = pl.DeviceIdType.MESH
F32 = jnp.float32
BF16 = jnp.bfloat16
L = 128


def phi(jobs, coef, quad, first, last):
    tiles = jobs[0][0].shape[1]
    lane = lax.broadcasted_iota(jnp.int32, (8, L), 1)
    low, high = lane == 0, lane == L - 1
    cache = {}

    def load(job, b, sp, c):
        key = (job, b, sp, c)
        if key not in cache:
            x = jobs[job][0][sp, c, H + b * 8 : H + b * 8 + 8, :]
            cache[key] = (x, pltpu.roll(x, 1, 1), pltpu.roll(x, L - 1, 1))
        return cache[key]

    for blk in range(first, last):
        rows = slice(blk * 8, blk * 8 + 8)
        for c in range(tiles):
            cols = slice(c * L, c * L + L)
            k = [coef[i, rows, cols] for i in (0, 1, 2, 4)]
            q = [quad[i, rows, cols] for i in (0, 1)]
            for job, (_, emit) in enumerate(jobs):
                x, around = [], []
                for sp in range(2):
                    v, left, right = load(job, blk, sp, c)
                    at = H + blk * 8
                    above = jobs[job][0][sp, c, at - 1 : at + 7, :]
                    below = jobs[job][0][sp, c, at + 1 : at + 9, :]
                    left = jnp.where(low, load(job, blk, sp, c - 1)[1] if c > 0 else 0.0, left)
                    right = jnp.where(high, load(job, blk, sp, c + 1)[2] if c < tiles - 1 else 0.0, right)
                    x.append(v)
                    around.append((above + below) + (left + right))
                r = k[3] * x[0] * (x[1] * x[1])
                emit(0, rows, cols, q[0] * x[0] + k[0] * around[0] + (k[2] - r))
                emit(1, rows, cols, q[1] * x[1] + k[1] * around[1] + r)


def put(dst, sp, rows, cols, value):
    dst[sp, cols.start // L, rows.start + H : rows.stop + H, :] = value


def into(dst):
    return lambda sp, rows, cols, value: put(dst, sp, rows, cols, value)


def tiled(dst, src):
    for sp in range(2):
        x = src[sp]
        for c in range(dst.shape[1]):
            dst[sp, c, H : H + x.shape[0], :] = x[:, c * L : c * L + L]


def flat(src, rows):
    rows = slice(rows.start + H, rows.stop + H)
    tiles = src.shape[1]
    return [
        jnp.concatenate([src[sp, c, rows, :] for c in range(tiles)], 1) if tiles > 1 else src[sp, 0, rows, :]
        for sp in range(2)
    ]


def times(x, matrix):
    n = x.shape[0]
    a = x.astype(BF16)
    r = x - a.astype(F32)
    b = r.astype(BF16)
    c = (r - b.astype(F32)).astype(BF16)
    y = jnp.dot(jnp.concatenate([a, b, c], 0), matrix, preferred_element_type=F32)
    return y[:n] + y[n : 2 * n] + y[2 * n :]


def coarsen(xs, wide, cmat, scr):
    rows, cols = xs[0].shape
    pad = H if wide else 0
    span = rows + 2 * pad
    y = times(jnp.concatenate(xs, 0), cmat[0:cols, 0 : cols // 2])
    tiles = cols // 2 // L
    for k in range(len(xs)):
        for c in range(tiles):
            at = k * span + pad
            scr[c, at : at + rows, :] = y[k * rows : (k + 1) * rows, c * L : c * L + L]
            if pad:
                scr[c, at - pad : at, :] = jnp.zeros((pad, L), F32)
                scr[c, at + rows : at + rows + pad, :] = jnp.zeros((pad, L), F32)
    out = []
    for k in range(len(xs)):
        parts = [
            scr[c, pl.ds(k * span, span // 2, stride=2), :] + scr[c, pl.ds(k * span + 1, span // 2, stride=2), :]
            for c in range(tiles)
        ]
        out.append(0.25 * (jnp.concatenate(parts, 1) if tiles > 1 else parts[0]))
    return out


def refine(xs, emat, scr):
    rows, cols = xs[0].shape
    tiles = cols // L
    span = 2 * rows
    for k, x in enumerate(xs):
        for c in range(tiles):
            for d in range(2):
                scr[c, pl.ds(k * span + d, rows, stride=2), :] = x[:, c * L : c * L + L]
    ys = []
    for k in range(len(xs)):
        parts = [scr[c, k * span + H : (k + 1) * span - H, :] for c in range(tiles)]
        ys.append(jnp.concatenate(parts, 1) if tiles > 1 else parts[0])
    z = times(jnp.concatenate(ys, 0), emat[0:cols, 0 : 2 * cols])
    n = span - 2 * H
    return [z[k * n : (k + 1) * n] for k in range(len(xs))]


def kernel(
    T, S,
    initial, guess, kappa, feed, kill, react, out,
    cf, q0, c1, q1, c2, q2, ga, gb, ca, cb, cc, st0, st1, sb0, sb1, outbuf,
    wa, wb, wc, gs, vs, vv, ps, pr, ei, eo, zz, zy, cmat, emat, scr,
    s_loc, r_cf, r_gb, r_ga, r_c1, r_ca, r_cb, r_vs, r_gs, r_e, r_d, s_out, s_send,
):
    t = lax.axis_index("tm")
    s = lax.axis_index("space")
    m = lax.rem(t, GROUP)
    base = t - m
    N = cf.shape[1] - 2 * H
    N1 = c1.shape[1] - 2 * H
    N2 = ei.shape[1] - 2 * H
    has = {-1: s > 0, 1: s < S - 1}
    opening = t == 0
    further = t < T - 1
    first = m == 0
    follows = base > 0
    leads = t + GROUP < T
    partner = m + 1 - 2 * lax.rem(m, 2)
    across = lax.rem(m + 2, GROUP)
    distant = lax.rem(partner + 2, GROUP)
    sends = []
    number = [0]

    def edge(n, ds):
        if ds == -1:
            return slice(0, H), slice(n + H, n + 2 * H)
        if ds == 1:
            return slice(n - H, n), slice(0, H)
        return slice(0, n), slice(H, n + H)

    def shift(sl, by):
        return slice(sl.start + by, sl.stop + by)

    def begin(cond, copies):
        made = []
        for src, dst, rsem, tt, ss in copies:
            made.append(pltpu.make_async_remote_copy(
                src_ref=src, dst_ref=dst, send_sem=s_send.at[number[0]], recv_sem=rsem,
                device_id=(tt, ss), device_id_type=MESH,
            ))
            number[0] += 1

        def go():
            for c in made:
                c.start()

        if cond is None:
            go()
        else:
            pl.when(cond)(go)
        sends.append((cond, made))

    def arrive(cond, waits):
        def go():
            for dst, rsem in waits:
                pltpu.make_async_copy(dst, dst, rsem).wait()

        if cond is None:
            go()
        else:
            pl.when(cond)(go)

    mid = slice(H, N + H)
    inner = slice(H, N1 + H)
    core = slice(H, N2 + H)
    local = [
        pltpu.make_async_copy(guess.at[SPAN - 1], gb.at[:, mid], s_loc.at[0]),
        pltpu.make_async_copy(kappa, cf.at[0:2, mid], s_loc.at[1]),
        pltpu.make_async_copy(feed, cf.at[2, mid], s_loc.at[2]),
        pltpu.make_async_copy(kill, cf.at[3, mid], s_loc.at[3]),
        pltpu.make_async_copy(react, cf.at[4, mid], s_loc.at[4]),
    ]
    for c in local:
        c.start()
    opened = [
        pltpu.make_async_copy(initial, ga.at[:, mid], s_loc.at[5]),
        pltpu.make_async_copy(initial, ca.at[:, mid], s_loc.at[6]),
    ]

    @pl.when(opening)
    def _():
        for c in opened:
            c.start()

    for ds in (-1, 1):
        @pl.when(jnp.logical_not(has[ds]))
        def _():
            for ref, n in ((cf, N), (ga, N), (gb, N), (ca, N), (cb, N), (c1, N1), (vs, N1)):
                rows = slice(0, H) if ds == -1 else slice(n + H, n + 2 * H)
                ref[:, rows, :] = jnp.zeros((ref.shape[0], H, ref.shape[2]), F32)
            rows = slice(0, H) if ds == -1 else slice(N1 + H, N1 + 2 * H)
            gs[:, :, rows, :] = jnp.zeros((SPAN, 2, H, gs.shape[3]), F32)
            pr[(1 - ds) // 2] = jnp.zeros(pr.shape[1:], F32)
            rows = slice(0, H) if ds == -1 else slice(N2 + H, N2 + 2 * H)
            ei[:, rows, :] = jnp.zeros((2, H, ei.shape[2]), F32)

    @pl.when(base == 0)
    def _():
        ei[...] = jnp.zeros(ei.shape, F32)

    barrier = pltpu.get_barrier_semaphore()
    count = jnp.int32(0)
    known = []
    for dt in (-GROUP, -1, 0, 1, GROUP):
        known.append((t + dt, (t + dt >= 0) & (t + dt < T), dt == 0))
    known.append((base + across, t >= 0, False))
    far = GROUP - 1 - m
    known.append((base + far, (m == 0) | (m == GROUP - 1), False))
    for other, there, own in known:
        for ds in (-1, 0, 1):
            if own and ds == 0:
                continue
            cond = there & has[ds] if ds else there

            @pl.when(cond)
            def _():
                pl.semaphore_signal(barrier, inc=1, device_id=(other, s + ds), device_id_type=MESH)

            count = count + cond.astype(jnp.int32)

    pl.semaphore_wait(barrier, count)

    for ds in (-1, 1):
        src, dst = edge(N, ds)
        k = (ds + 1) // 2
        begin(has[ds], [
            (guess.at[SPAN - 1, :, src], gb.at[:, dst], r_gb.at[k], t, s + ds),
            (kappa.at[:, src], cf.at[0:2, dst], r_cf.at[k, 0], t, s + ds),
            (feed.at[src], cf.at[2, dst], r_cf.at[k, 1], t, s + ds),
            (kill.at[src], cf.at[3, dst], r_cf.at[k, 2], t, s + ds),
            (react.at[src], cf.at[4, dst], r_cf.at[k, 3], t, s + ds),
        ])
    begin(further, [(guess.at[2 * SPAN - 1], ga.at[:, mid], r_ga.at[1], t + 1, s)])

    ii = lax.broadcasted_iota(jnp.int32, cmat.shape, 0) - 2 * lax.broadcasted_iota(jnp.int32, cmat.shape, 1)
    cmat[...] = jnp.where((ii == 0) | (ii == 1), 1.0, 0.0).astype(BF16)
    jj = lax.broadcasted_iota(jnp.int32, emat.shape, 1) - 2 * lax.broadcasted_iota(jnp.int32, emat.shape, 0)
    emat[...] = jnp.where((jj == 0) | (jj == 1), 1.0, 0.0).astype(BF16)
    eo[...] = jnp.zeros(eo.shape, F32)
    for ref, n in ((st0, N), (st1, N), (sb0, N), (sb1, N), (vv, N1), (zz, N2), (zy, N2)):
        for at in (0, n + 3 * H):
            ref[..., at : at + H, :] = jnp.zeros(ref.shape[:-2] + (H, L), F32)

    for c in local:
        c.wait()
    scale = (2.0, 2.0, 8.0, 8.0, 8.0)
    for k, x in enumerate(coarsen([cf[k, mid, :] for k in range(5)], False, cmat, scr)):
        c1[k, inner, :] = scale[k] * x
    for k, x in enumerate(coarsen([c1[k, inner, :] for k in range(5)], False, cmat, scr)):
        c2[k, core, :] = scale[k] * x
    q2[0, core, :] = 1.0 - c2[2, core, :] - 4.0 * c2[0, core, :]
    q2[1, core, :] = 1.0 - (c2[2, core, :] + c2[3, core, :]) - 4.0 * c2[1, core, :]

    for ds in (-1, 1):
        k = (ds + 1) // 2
        dst = edge(N, ds)[1]
        arrive(has[-ds], [
            (gb.at[:, dst], r_gb.at[k]),
            (cf.at[0:2, dst], r_cf.at[k, 0]),
            (cf.at[2, dst], r_cf.at[k, 1]),
            (cf.at[3, dst], r_cf.at[k, 2]),
            (cf.at[4, dst], r_cf.at[k, 3]),
        ])
    for ds in (-1, 1):
        src, dst = edge(N, ds)
        src1, dst1 = edge(N1, ds)
        begin(further & has[ds], [
            (guess.at[2 * SPAN - 1, :, src], ga.at[:, dst], r_ga.at[ds + 1], t + 1, s + ds),
        ])
        begin(opening & has[ds], [
            (initial.at[:, src], ga.at[:, dst], r_ga.at[ds + 1], t, s + ds),
            (initial.at[:, src], ca.at[:, dst], r_ca.at[ds + 1], t, s + ds),
        ])
        begin(has[ds], [
            (c1.at[:, shift(src1, H)], c1.at[:, dst1], r_c1.at[(ds + 1) // 2], t, s + ds),
        ])

    def quads(coef, quad):
        quad[0] = 1.0 - coef[2] - 4.0 * coef[0]
        quad[1] = 1.0 - (coef[2] + coef[3]) - 4.0 * coef[1]

    quads(cf, q0)
    blocks = (N + 2 * H) // 8

    def interval(src):
        tiled(st1, src)

        @pl.loop(0, SPAN // 2)
        def _(_):
            phi([(st1, into(st0))], cf, q0, 0, blocks)
            phi([(st0, into(st1))], cf, q0, 0, blocks)

    interval(gb)
    for sp, x in enumerate(flat(st1, mid)):
        cc[sp] = x
    begin(further, [(cc, ca.at[:, mid], r_ca.at[1], t + 1, s)])
    for ds in (-1, 1):
        src, dst = edge(N, ds)
        begin(further & has[ds], [(cc.at[:, src], ca.at[:, dst], r_ca.at[ds + 1], t + 1, s + ds)])

    @pl.when(opening)
    def _():
        for c in opened:
            c.wait()

    arrive(jnp.logical_not(opening), [(ga.at[:, mid], r_ga.at[1])])
    for ds in (-1, 1):
        arrive(has[-ds], [(ga.at[:, edge(N, ds)[1]], r_ga.at[ds + 1])])
    interval(ga)
    for sp, x in enumerate(flat(st1, mid)):
        cb[sp, mid, :] = x
    for ds in (-1, 1):
        src, dst = edge(N, ds)
        begin(has[ds], [(cb.at[:, shift(src, H)], cb.at[:, dst], r_cb.at[(ds + 1) // 2], t, s + ds)])

    arrive(jnp.logical_not(opening), [(ca.at[:, mid], r_ca.at[1])])
    for ds in (-1, 1):
        arrive(has[-ds], [
            (ca.at[:, edge(N, ds)[1]], r_ca.at[ds + 1]),
            (c1.at[:, edge(N1, ds)[1]], r_c1.at[(ds + 1) // 2]),
        ])
    quads(c1, q1)
    blocks1 = (N1 + 2 * H) // 8
    for k, x in enumerate(coarsen([ca[0], ca[1]], True, cmat, scr)):
        wa[k] = x

    @pl.when(first)
    def _():
        vs[:, inner, :] = wa[:, inner, :]

    begin(first, [(wa.at[:, inner], vs.at[:, inner], r_vs.at[1], base + r, s) for r in range(1, GROUP)])
    for ds in (-1, 1):
        src, dst = edge(N1, ds)
        begin(first & has[ds], [
            (wa.at[:, shift(src, H)], vs.at[:, dst], r_vs.at[ds + 1], base + r, s + ds) for r in range(GROUP)
        ])

    def forcing(which, w, r):
        slot = 2 * m + which
        last = jnp.where(m == GROUP - 1, 1.0, 0.0) if which else None

        def emit(sp, rows, cols, value):
            own = shift(rows, -H)
            g = r[sp][own, cols] - value
            if which:
                g = g - last * wc[sp, own, cols]
            gs[slot, sp, rows, cols] = g

        tiled(vv.at[SPAN], w)
        phi([(vv.at[SPAN], emit)], c1, q1, 1, blocks1 - 1)
        begin(None, [
            (gs.at[slot, :, inner], gs.at[slot, :, inner], r_gs.at[slot, 1], base + to, s)
            for to in (across, distant, partner)
        ])
        for ds in (-1, 1):
            src, dst = edge(N1, ds)
            begin(has[ds], [
                (gs.at[slot, :, shift(src, H)], gs.at[slot, :, dst], r_gs.at[slot, ds + 1], base + to, s + ds)
                for to in (across, distant, partner, m)
            ])

    interval(ca)
    forcing(0, wa, coarsen(flat(st1, mid), False, cmat, scr))
    for k, x in enumerate(coarsen([cc[0], cc[1]], False, cmat, scr)):
        wc[k] = x
    for ds in (-1, 1):
        arrive(has[-ds], [(cb.at[:, edge(N, ds)[1]], r_cb.at[(ds + 1) // 2])])
    for k, x in enumerate(coarsen([cb[0], cb[1]], True, cmat, scr)):
        wb[k] = x
    interval(cb)
    forcing(1, wb, coarsen(flat(st1, mid), False, cmat, scr))

    arrive(jnp.logical_not(first), [(vs.at[:, inner], r_vs.at[1])])
    for ds in (-1, 1):
        arrive(has[-ds], [(vs.at[:, edge(N1, ds)[1]], r_vs.at[ds + 1])])
    tiled(vv.at[0], vs)
    for sp, x in enumerate(coarsen([vs[0], vs[1]], True, cmat, scr)):
        zz[sp, 0, H : H + x.shape[0], :] = x
    top = (N2 + 2 * H) // 8

    def emit_old(sp, rows, cols, value):
        eo[sp, rows, cols] = -value

    def emit_new(sp, rows, cols, value):
        eo[sp, rows, cols] = eo[sp, rows, cols] + value

    phi([(zz, emit_old)], c2, q2, 1, top - 1)

    for which in range(2):
        for other in (m, partner, across, distant):
            slot = 2 * other + which
            if other is not m:
                arrive(None, [(gs.at[slot, :, inner], r_gs.at[slot, 1])])
    for ds in (-1, 1):
        arrive(has[-ds], [(gs.at[i, :, edge(N1, ds)[1]], r_gs.at[i, ds + 1]) for i in range(SPAN)])

    def sweep(count):
        @pl.loop(0, count)
        def _(i):
            def emit(sp, rows, cols, value):
                put(vv.at[i + 1], sp, rows, cols, value + gs[i, sp, rows, cols])

            phi([(vv.at[i], emit)], c1, q1, 0, blocks1)

    sweep(SPAN)

    r = coarsen(flat(vv.at[SPAN], inner), False, cmat, scr)
    arrive(follows, [(ei.at[:, core], r_e.at[1])])
    for ds in (-1, 1):
        arrive(follows & has[-ds], [(ei.at[:, edge(N2, ds)[1]], r_e.at[ds + 1])])
    for sp in range(2):
        zy[sp, 0, H : H + ei.shape[1], :] = zz[sp, 0, H : H + ei.shape[1], :] + ei[sp]
    phi([(zy, emit_new)], c2, q2, 1, top - 1)
    for sp in range(2):
        eo[sp, core, :] = eo[sp, core, :] + r[sp]
    begin(leads, [(eo.at[:, core], ei.at[:, core], r_e.at[1], t + GROUP, s)])
    for ds in (-1, 1):
        src, dst = edge(N2, ds)
        begin(leads & has[ds], [
            (eo.at[:, shift(src, H)], ei.at[:, dst], r_e.at[ds + 1], t + GROUP, s + ds),
        ])

    p = refine([ei[0], ei[1]], emat, scr)
    for sp in range(2):
        p[sp] = vs[sp] + p[sp]
    tiled(vv.at[0], p)
    sweep(SPAN - 1)
    da = [x - wa[sp, inner, :] for sp, x in enumerate(flat(vv.at[2 * m], inner))]
    db = [x - wb[sp, inner, :] for sp, x in enumerate(flat(vv.at[2 * m + 1], inner))]
    half = H // 2
    for sp in range(2):
        ps[0, sp] = jnp.concatenate([da[sp][0:half], db[sp][0:half]], 0)
        ps[1, sp] = jnp.concatenate([da[sp][N1 - half :], db[sp][N1 - half :]], 0)
    for ds in (-1, 1):
        k = (ds + 1) // 2
        begin(has[ds], [(ps.at[k], pr.at[k], r_d.at[k], t, s + ds)])

    def done(i):
        return pltpu.make_async_copy(outbuf.at[i], out.at[i], s_out.at[i])

    p = refine([eo[0], eo[1]], emat, scr)
    for sp in range(2):
        x = wc[sp] + p[sp][inner]
        for c in range(vv.shape[2]):
            vv[SPAN, sp, c, 2 * H : 2 * H + N1, :] = x[:, c * L : c * L + L]
    zeros = jnp.zeros((H, c1.shape[2]), F32)
    last = flat(vv.at[2 * m + 2], inner)
    tail = [jnp.concatenate([zeros, last[sp] - wc[sp], zeros], 0) for sp in range(2)]
    p = refine(tail, emat, scr)
    for sp in range(2):
        outbuf[2 * SPAN - 1, sp] = cc[sp] + p[sp][mid]
    done(2 * SPAN - 1).start()

    for ds in (-1, 1):
        k = (ds + 1) // 2
        arrive(has[-ds], [(pr.at[k], r_d.at[k])])
    zeros = jnp.zeros((half, c1.shape[2]), F32)
    delta = []
    for which, d in enumerate((da, db)):
        rows = slice(which * half, which * half + half)
        for sp in range(2):
            delta.append(jnp.concatenate([zeros, pr[1, sp, rows, :], d[sp], pr[0, sp, rows, :], zeros], 0))
    p = refine(delta, emat, scr)
    for sp in range(2):
        u = cb[sp] + p[2 + sp]
        for c in range(st1.shape[1]):
            st1[sp, c, H : H + u.shape[0], :] = ca[sp, :, c * L : c * L + L] + p[sp][:, c * L : c * L + L]
            sb1[sp, c, H : H + u.shape[0], :] = u[:, c * L : c * L + L]
        outbuf[SPAN - 1, sp] = u[mid]
    done(SPAN - 1).start()

    def step(sources, targets, i):
        def emits(dst, at):
            def emit(sp, rows, cols, value):
                put(dst, sp, rows, cols, value)
                if H <= rows.start < N + H:
                    outbuf[at, sp, shift(rows, -H), cols] = value

            return emit

        at = (i, SPAN + i)
        phi([(sources[j], emits(targets[j], at[j])) for j in range(2)], cf, q0, 0, blocks)
        for j in range(2):
            done(at[j]).start()

    @pl.loop(0, 3)
    def _(k):
        step((st1, sb1), (st0, sb0), 2 * k)
        step((st0, sb0), (st1, sb1), 2 * k + 1)

    step((st1, sb1), (st0, sb0), SPAN - 2)
    for i in range(2 * SPAN):
        done(i).wait()
    for cond, made in sends:
        def settle():
            for c in made:
                c.wait_send()

        if cond is None:
            settle()
        else:
            pl.when(cond)(settle)


def local(T, S, initial, guess, kappa, feed, kill, react):
    _, N, C = initial.shape
    W, W1, W2 = N + 2 * H, N // 2 + 2 * H, N // 4 + 2 * H
    C1, C2 = C // 2, C // 4
    V = lambda *shape: pltpu.VMEM(shape, F32)
    D = lambda *shape: pltpu.SemaphoreType.DMA(shape)
    scratch = [
        V(5, W, C), V(2, W, C), V(5, W1, C1), V(2, W1, C1), V(5, W2, C2), V(2, W2, C2),
        V(2, W, C), V(2, W, C), V(2, W, C), V(2, W, C), V(2, N, C),
        *[V(2, C // L, W + 2 * H, L) for _ in range(4)], V(2 * SPAN, 2, N, C),
        V(2, W1, C1), V(2, W1, C1), V(2, N // 2, C1), V(SPAN, 2, W1, C1), V(2, W1, C1),
        V(SPAN + 1, 2, C1 // L, W1 + 2 * H, L), V(2, 2, H, C1), V(2, 2, H, C1), V(2, W2, C2), V(2, W2, C2),
        V(2, C2 // L, W2 + 2 * H, L), V(2, C2 // L, W2 + 2 * H, L), pltpu.VMEM((C, C1), BF16), pltpu.VMEM((C1, C), BF16), V(C1 // L, 8 * W1, L),
        D(7), D(2, 4), D(2), D(3), D(2), D(3), D(2), D(3), D(SPAN, 3), D(3), D(2),
        D(2 * SPAN), D(96),
    ]

    def body(*refs):
        kernel(T, S, *refs)

    return pl.pallas_call(
        body,
        out_shape=jax.ShapeDtypeStruct(guess.shape, F32),
        in_specs=[pl.BlockSpec(memory_space=pltpu.HBM)] * 6,
        out_specs=pl.BlockSpec(memory_space=pl.ANY),
        scratch_shapes=scratch,
        compiler_params=pltpu.CompilerParams(
            collective_id=0, has_side_effects=True, vmem_limit_bytes=48 * 1024 * 1024
        ),
    )(*[pltpu.with_memory_space_constraint(x, pltpu.HBM) for x in (initial, guess, kappa, feed, kill, react)])


def solution(mesh):
    T, S = mesh.shape["tm"], mesh.shape["space"]
    in_specs = (
        P(None, "space", None),
        P("tm", None, "space", None),
        P(None, "space", None),
        P("space", None),
        P("space", None),
        P("space", None),
    )
    out_specs = P("tm", None, "space", None)

    def run(*args):
        return local(T, S, *args)

    return jax.shard_map(run, mesh=mesh, in_specs=in_specs, out_specs=out_specs, check_vma=False)
```
